128 devices in a mesh: sec: 32 (over y_lo, x, z), tile: 4 (over y_hi, core).
Axes of the slice: x: 4, y: 4 (y_hi: 2, y_lo: 2; y = y_hi * 2 + y_lo), z: 4, core: 2. Of those that a mesh axis runs over, the one named last changes fastest.
Arguments:
- displacement: float32 [2, 32, 1024, 2048], P(None, 'sec', 'tile'), may hold values from -6 to 6
- spring: float32 [32, 1024, 2048], P('sec', 'tile'), may hold values from 0.5 to 2
- stiff_table: float32 [8], replicated, may hold values from 0.25 to 2
- match_blocks: int32 [2, 32, 1024], P(None, 'sec', 'tile'), may hold values from 0 to 4095
- match_class: int32 [32, 1024], P('sec', 'tile'), may hold values from 0 to 7
Outputs:
- relaxed: float32 [2, 32, 1024, 2048], P(None, 'sec', 'tile')
The draws below stay inside these ranges and needn't reach their ends.
All inputs are finite; a program needn't handle non-finite values.
Results may differ from the reference program's by a relative error of at most 0.000053.
Values sent between devices are 32-bit elements; how exact they have to be, the bound alone decides.
A program may use at most 128 MiB of HBM per device.

```python
import math
import jax
import jax.numpy as jnp

R_DEV = 256
COLS = 2048
MAXM = 256
NCLASS = 8
ITERS = 3
NSEC = 32
ROWS = 1024
NBLK = 4096
N_TILE = 4


def plant(array, key, low, top_value):
    place = [jax.random.randint(jax.random.fold_in(key, axis), (), 0, length) for axis, length in enumerate(array.shape)]
    widest = array.shape.index(max(array.shape))
    beside = place[:widest] + [(place[widest] + 1) % array.shape[widest]] + place[widest + 1:]
    return array.at[tuple(place)].set(low).at[tuple(beside)].set(top_value)


def steps_of(rng, dims, split, least, high):
    def one(dim, blocks):
        draws = jax.random.uniform(jax.random.fold_in(jax.random.fold_in(rng, 6), dim), (blocks,), jnp.float32, least / len(split), high / len(split))
        return jnp.repeat(jnp.exp(draws), dims[dim] // blocks).reshape((-1,) + (1,) * (len(dims) - dim - 1))

    gain = one(*split[0])
    for cut in split[1:]:
        gain = gain * one(*cut)
    return gain


def normal_values(stream_key, extent, spread, limit, cuts=(), kind=jnp.bfloat16):
    gain = steps_of(stream_key, extent, cuts, -0.22, 0.18) if cuts else 1.0
    values = jax.random.normal(stream_key, extent, jnp.float32) * spread * gain
    return jnp.minimum(jnp.maximum(values, -limit), limit).astype(kind)


def setup_inputs(seed: int = 0) -> dict:
    streams_of = jax.random.split(jax.random.key(seed), 6)
    return {
        "displacement": normal_values(streams_of[0], (2, NSEC, ROWS, COLS), 1.0, 6.0, ((1, 32), (2, 4)), jnp.float32),
        "spring": jnp.clip(jnp.exp(math.log(2.0) - 1.3862944 * jax.random.uniform(streams_of[1], (NSEC, ROWS, COLS), jnp.float32) ** steps_of(streams_of[1], (NSEC, ROWS, COLS), ((0, 32), (1, 4)), -0.2, 0.2)), 0.5, 2.0),
        "stiff_table": jnp.clip(jnp.exp(jax.random.uniform(streams_of[2], (NCLASS,), jnp.float32, math.log(0.25), math.log(2.0))), 0.25, 2.0),
        "match_blocks": plant(jax.random.randint(streams_of[3], (2, NSEC, N_TILE * MAXM), 0, NBLK), jax.random.fold_in(streams_of[3], 1), 0, NBLK - 1).astype(jnp.int32),
        "match_class": plant(jax.random.randint(streams_of[4], (NSEC, N_TILE * MAXM), 0, NCLASS), jax.random.fold_in(streams_of[4], 1), 0, NCLASS - 1).astype(jnp.int32),
    }


def reference(displacement, spring, stiff_table, match_blocks, match_class):
    block_count = R_DEV * COLS // 128
    sections = jnp.arange(NSEC, dtype=jnp.int32)[:, None, None]
    bands = jnp.arange(N_TILE, dtype=jnp.int32)[None, :, None]
    source = match_blocks[0].reshape(NSEC, N_TILE, MAXM)
    target = match_blocks[1].reshape(NSEC, N_TILE, MAXM)
    classes_in = match_class.reshape(NSEC, N_TILE, MAXM)
    alive = (sections < NSEC - 1).astype(jnp.float32)
    coupling = (stiff_table[classes_in] * alive).reshape(-1)
    following = jnp.minimum(sections + 1, NSEC - 1)
    global_source = ((sections * N_TILE + bands) * block_count + source).reshape(-1).astype(jnp.int32)
    global_target = ((following * N_TILE + bands) * block_count + target).reshape(-1).astype(jnp.int32)
    total_blocks = NSEC * N_TILE * block_count
    diag_blocks = jnp.zeros((total_blocks,), jnp.float32).at[global_source].add(coupling).at[global_target].add(coupling)
    diagonal = 4.0 * spring + jnp.repeat(diag_blocks.reshape(NSEC, ROWS, COLS // 128), 128, axis=2)
    field = displacement
    for sweep in range(ITERS):
        blocked = field.reshape(2, total_blocks, 128)
        at_source = blocked[:, global_source]
        at_target = blocked[:, global_target]
        term_match = coupling[None, :, None] * (at_target - at_source)
        matched = jnp.zeros_like(blocked).at[:, global_source].add(term_match).at[:, global_target].add(-term_match)
        padded = jnp.pad(field, ((0, 0), (0, 0), (1, 1), (1, 1)))
        laplace = padded[:, :, 2:, 1:-1] + padded[:, :, :-2, 1:-1] + padded[:, :, 1:-1, 2:] + padded[:, :, 1:-1, :-2] - 4.0 * field
        force = spring[None] * laplace + matched.reshape(field.shape)
        field = field + 0.8 * force / diagonal[None]
    return field
```

```python
import functools

import jax
import jax.numpy as jnp
from jax import lax
from jax.experimental import pallas as pl
from jax.experimental.pallas import tpu as pltpu
from jax.sharding import PartitionSpec as P

ITERS = 3
LANES = 128
PAD = 8
CHUNKS = 2
STRIP = 64
MESH = pl.DeviceIdType.MESH
F32 = jnp.float32
BF16 = jnp.bfloat16


def split(value):
    high = value.astype(BF16)
    return high, (value - high.astype(F32)).astype(BF16)


def kernel(
    disp, spring, table, blocks, classes, out,
    f_a, f_b, spr, a_ref, g_ref, onehot, pmat,
    own_index, prev_index, own_blocks, prev_blocks, own_class, prev_class,
    block_cols, cmat, gathered_g, gathered_l, sent, received, t_high, t_low,
    edge_out, edge_in,
    load_sem, spring_sem, list_sem, list_send, list_recv,
    row_send, row_recv, edge_send, edge_recv, out_sem,
):
    fields, _, height, breadth = disp.shape
    columns = breadth // LANES
    matches = classes.shape[1]
    part = matches // CHUNKS
    section, sections = lax.axis_index("sec"), lax.axis_size("sec")
    tile, tiles = lax.axis_index("tile"), lax.axis_size("tile")
    following = lax.rem(section + 1, sections)
    previous = lax.rem(section + sections - 1, sections)
    has_upper, has_lower = tile > 0, tile < tiles - 1

    barrier = pltpu.get_barrier_semaphore()
    for peer in (following, previous):
        pl.semaphore_signal(barrier, inc=1, device_id={"sec": peer}, device_id_type=MESH)

    @pl.when(has_upper)
    def _():
        pl.semaphore_signal(barrier, inc=1, device_id={"tile": tile - 1}, device_id_type=MESH)

    @pl.when(has_lower)
    def _():
        pl.semaphore_signal(barrier, inc=1, device_id={"tile": tile + 1}, device_id_type=MESH)

    rows = pl.ds(PAD, height)

    def load_field(cb):
        lanes = pl.ds(pl.multiple_of(cb * LANES, LANES), LANES)
        return pltpu.make_async_copy(disp.at[:, 0, :, lanes], f_a.at[:, cb + 1, rows, :], load_sem.at[cb])

    def load_spring(cb):
        lanes = pl.ds(pl.multiple_of(cb * LANES, LANES), LANES)
        return pltpu.make_async_copy(spring.at[0, :, lanes], spr.at[cb], spring_sem.at[cb])

    own_lists = [
        pltpu.make_async_copy(blocks.at[0], own_index, list_sem.at[0]),
        pltpu.make_async_copy(blocks.at[0], own_blocks, list_sem.at[1]),
        pltpu.make_async_copy(classes, own_class, list_sem.at[2]),
    ]
    for copy in own_lists:
        copy.start()

    def start_loads(cb, carry):
        load_field(cb).start()
        return carry

    lax.fori_loop(0, columns, start_loads, 0)

    def start_springs(cb, carry):
        load_spring(cb).start()
        return carry

    lax.fori_loop(0, columns, start_springs, 0)

    for field in (f_a, f_b):
        for cb in (0, columns + 1):
            field[:, cb] = jnp.zeros((fields, height + 2 * PAD, LANES), F32)
        field[:, :, 0:PAD] = jnp.zeros((fields, columns + 2, PAD, LANES), F32)
        field[:, :, PAD + height :] = jnp.zeros((fields, columns + 2, PAD, LANES), F32)

    pl.semaphore_wait(barrier, 2 + has_upper.astype(jnp.int32) + has_lower.astype(jnp.int32))

    list_copies = [
        pltpu.make_async_remote_copy(
            src_ref=src, dst_ref=dst, send_sem=list_send.at[i], recv_sem=list_recv.at[i],
            device_id={"sec": following}, device_id_type=MESH,
        )
        for i, (src, dst) in enumerate(((blocks.at[1], prev_blocks), (classes, prev_class)))
    ]
    for copy in list_copies:
        copy.start()

    def edge_copies(step):
        upward = pltpu.make_async_remote_copy(
            src_ref=edge_out.at[step, 0], dst_ref=edge_in.at[step, 1],
            send_sem=edge_send.at[step, 0], recv_sem=edge_recv.at[step, 1],
            device_id={"tile": tile - 1}, device_id_type=MESH,
        )
        downward = pltpu.make_async_remote_copy(
            src_ref=edge_out.at[step, 1], dst_ref=edge_in.at[step, 0],
            send_sem=edge_send.at[step, 1], recv_sem=edge_recv.at[step, 0],
            device_id={"tile": tile + 1}, device_id_type=MESH,
        )
        return upward, downward

    def row_copy(step, side, chunk):
        mine = side * matches + chunk * part
        theirs = (1 - side) * matches + chunk * part
        return pltpu.make_async_remote_copy(
            src_ref=sent.at[step, :, pl.ds(mine, part), :],
            dst_ref=received.at[step, :, pl.ds(theirs, part), :],
            send_sem=row_send.at[step, side, chunk],
            recv_sem=row_recv.at[step, 1 - side, chunk],
            device_id={"sec": (following, previous)[side]}, device_id_type=MESH,
        )

    def row_arrival(step, side, chunk):
        mine = side * matches + chunk * part
        return pltpu.make_async_remote_copy(
            src_ref=sent.at[step, :, pl.ds(mine, part), :],
            dst_ref=received.at[step, :, pl.ds(mine, part), :],
            send_sem=row_send.at[step, side, chunk],
            recv_sem=row_recv.at[step, side, chunk],
            device_id={"sec": (following, previous)[side]}, device_id_type=MESH,
        )

    def place(block):
        return block % columns, block // columns

    def gather_rows(index, first, count, base, put):
        def group(g, carry):
            at = pl.multiple_of(first + g * 8, 8)
            for j in range(8):
                cb, row = place(index[0, at + j])
                put(base + at + j, cb, row)
            return carry

        lax.fori_loop(0, count // 8, group, 0)

    def put_sent(field):
        def put(at, cb, row):
            for c in range(fields):
                sent[0, c, pl.ds(at, 1), :] = field[c, cb + 1, pl.ds(PAD + row, 1), :]
        return put

    def put_l(field):
        def put(at, cb, row):
            for c in range(fields):
                gathered_l[c, pl.ds(at, 1), :] = field[c, cb + 1, pl.ds(PAD + row, 1), :]
        return put

    def put_g(at, cb, row):
        gathered_g[pl.ds(at, 1), :] = g_ref[cb, pl.ds(row, 1), :]

    own_lists[0].wait()

    def wait_loads(cb, carry):
        load_field(cb).wait()
        return carry

    lax.fori_loop(0, columns, wait_loads, 0)
    for chunk in range(CHUNKS):
        gather_rows(own_index, chunk * part, part, 0, put_sent(f_a))
        row_copy(0, 0, chunk).start()
    for copy in list_copies:
        copy.wait_recv()
    to_scalar = pltpu.make_async_copy(prev_blocks, prev_index, list_sem.at[0])
    to_scalar.start()

    def send_edges(step, field):
        def one(cb, carry):
            for c in range(fields):
                at = pl.ds(c * columns + cb, 1)
                edge_out[step, 0, at, :] = field[c, cb + 1, PAD : PAD + 1, :]
                edge_out[step, 1, at, :] = field[c, cb + 1, PAD + height - 1 : PAD + height, :]
            return carry

        lax.fori_loop(0, columns, one, 0)
        upward, downward = edge_copies(step)

        @pl.when(has_upper)
        def _():
            upward.start()

        @pl.when(has_lower)
        def _():
            downward.start()

    to_scalar.wait()
    for chunk in range(CHUNKS):
        gather_rows(prev_index, chunk * part, part, matches, put_sent(f_a))
        row_copy(0, 1, chunk).start()
    send_edges(0, f_a)

    own_lists[1].wait()
    own_lists[2].wait()
    lane = lax.broadcasted_iota(jnp.int32, (STRIP, LANES), 1)
    block_rows = []
    for side, (index_ref, class_ref, alive) in enumerate(
        ((own_blocks, own_class, section < sections - 1), (prev_blocks, prev_class, section > 0))
    ):
        index = index_ref[...].astype(F32)
        kind = class_ref[...]
        stiff = jnp.zeros(kind.shape, F32)
        for level in range(table.shape[0]):
            stiff = jnp.where(kind == level, table[level], stiff)
        stiff = stiff * jnp.where(alive, 1.0, 0.0)
        half = pl.ds(side * matches, matches)
        block_cols[half, :] = jnp.transpose(jnp.broadcast_to(index, (LANES, matches)))
        cmat[half, :] = jnp.transpose(jnp.broadcast_to(stiff, (LANES, matches)))
        block_rows.append(index)

    def fill_pmat(g, carry):
        at = pl.ds(pl.multiple_of(g * STRIP, STRIP), STRIP)
        col = block_cols[at, :]
        for side in range(2):
            for j in range(matches // LANES):
                row = block_rows[side][:, j * LANES : (j + 1) * LANES]
                first = side * matches + j * LANES
                pmat[at, first : first + LANES] = jnp.where(col == row, 1.0, 0.0).astype(BF16)
        return carry

    lax.fori_loop(0, 2 * matches // STRIP, fill_pmat, 0)

    def fill_onehot(g, carry):
        cb, strip = g // (height // STRIP), g % (height // STRIP)
        first = pl.multiple_of(strip * STRIP, STRIP)
        row = first + lax.broadcasted_iota(jnp.int32, (STRIP, LANES), 0)
        block = (row * columns + cb).astype(F32)
        for side in range(2):
            for j in range(matches // LANES):
                wanted = block_rows[side][:, j * LANES : (j + 1) * LANES]
                at = side * matches + j * LANES
                onehot[cb, pl.ds(first, STRIP), at : at + LANES] = jnp.where(block == wanted, 1.0, 0.0).astype(BF16)
        return carry

    lax.fori_loop(0, columns * (height // STRIP), fill_onehot, 0)

    c_high, c_low = split(cmat[...])
    c_parts = jnp.concatenate([c_high, c_low], axis=1)

    def fill_gain(cb, carry):
        load_spring(cb).wait()
        sums = jnp.dot(onehot[cb], c_parts, preferred_element_type=F32)
        stiff = spr[cb]
        gain = 0.8 / (4.0 * stiff + (sums[:, :LANES] + sums[:, LANES:]))
        g_ref[cb] = gain
        a_ref[cb] = gain * stiff
        return carry

    lax.fori_loop(0, columns, fill_gain, 0)
    gather_rows(own_index, 0, matches, 0, put_g)
    gather_rows(prev_index, 0, matches, matches, put_g)

    def stencil(field, result):
        def one(cb, carry):
            for s in range(height // STRIP):
                top = PAD + s * STRIP
                at = pl.ds(top, STRIP)
                a = a_ref[cb, s * STRIP : (s + 1) * STRIP]
                for c in range(fields):
                    here = field[c, cb + 1, at]
                    west, east = field[c, cb, at], field[c, cb + 2, at]
                    north = field[c, cb + 1, pl.ds(top - 1, STRIP)]
                    south = field[c, cb + 1, pl.ds(top + 1, STRIP)]
                    west = pltpu.roll(jnp.where(lane == LANES - 1, west, here), 1, axis=1)
                    east = pltpu.roll(jnp.where(lane == 0, east, here), LANES - 1, axis=1)
                    lap = ((north + south) + (west + east)) - 4.0 * here
                    result[c, cb + 1, at] = here + a * lap
            return carry

        lax.fori_loop(0, columns, one, 0)

    def add_edge(step, which, result):
        row = (0, height - 1)[which]

        def one(cb, carry):
            a = a_ref[cb, row : row + 1, :]
            for c in range(fields):
                at = pl.ds(c * columns + cb, 1)
                result[c, cb + 1, PAD + row : PAD + row + 1, :] += a * edge_in[step, which, at, :]
            return carry

        lax.fori_loop(0, columns, one, 0)

    def add_edges(step, result):
        upward, downward = edge_copies(step)

        @pl.when(has_upper)
        def _():
            pltpu.make_async_remote_copy(
                src_ref=edge_out.at[step, 0], dst_ref=edge_in.at[step, 0],
                send_sem=edge_send.at[step, 0], recv_sem=edge_recv.at[step, 0],
                device_id={"tile": tile - 1}, device_id_type=MESH,
            ).wait_recv()
            add_edge(step, 0, result)
            upward.wait_send()

        @pl.when(has_lower)
        def _():
            pltpu.make_async_remote_copy(
                src_ref=edge_out.at[step, 1], dst_ref=edge_in.at[step, 1],
                send_sem=edge_send.at[step, 1], recv_sem=edge_recv.at[step, 1],
                device_id={"tile": tile + 1}, device_id_type=MESH,
            ).wait_recv()
            add_edge(step, 1, result)
            downward.wait_send()

    def update(cb, result):
        sums = jnp.dot(onehot[cb], t_high[...], preferred_element_type=F32)
        sums = sums + jnp.dot(onehot[cb], t_low[...], preferred_element_type=F32)
        gain = g_ref[cb]
        for c in range(fields):
            result[c, cb + 1, rows, :] += gain * sums[:, c * LANES : (c + 1) * LANES]

    def store(cb, result):
        lanes = pl.ds(pl.multiple_of(cb * LANES, LANES), LANES)
        return pltpu.make_async_copy(result.at[:, cb + 1, rows, :], out.at[:, 0, :, lanes], out_sem.at[cb])

    field, result = f_a, f_b
    for step in range(ITERS):
        last = step == ITERS - 1
        stencil(field, result)
        add_edges(step, result)
        if not last:
            gather_rows(own_index, 0, matches, 0, put_l(result))
            gather_rows(prev_index, 0, matches, matches, put_l(result))
        for side in range(2):
            for chunk in range(CHUNKS):
                row_arrival(step, side, chunk).wait_recv()
                at = pl.ds(side * matches + chunk * part, part)
                c = cmat[at, :]
                for f in range(fields):
                    lanes = slice(f * LANES, (f + 1) * LANES)
                    high, low = split(c * (received[step, f, at, :] - sent[step, f, at, :]))
                    t_high[at, lanes] = high
                    t_low[at, lanes] = low
        if not last:
            for chunk in range(CHUNKS):
                for side in range(2):
                    at = pl.ds(side * matches + chunk * part, part)
                    sums = jnp.dot(pmat[at, :], t_high[...], preferred_element_type=F32)
                    sums = sums + jnp.dot(pmat[at, :], t_low[...], preferred_element_type=F32)
                    gain = gathered_g[at, :]
                    for f in range(fields):
                        lanes = slice(f * LANES, (f + 1) * LANES)
                        sent[step + 1, f, at, :] = gathered_l[f, at, :] + gain * sums[:, lanes]
                    row_copy(step + 1, side, chunk).start()

            def full(cb, carry):
                update(cb, result)
                return carry

            lax.fori_loop(0, columns, full, 0)
            send_edges(step + 1, result)
        else:

            def finish(cb, carry):
                update(cb, result)
                store(cb, result).start()
                return carry

            lax.fori_loop(0, columns, finish, 0)
        field, result = result, field

    for copy in list_copies:
        copy.wait_send()
    for step in range(ITERS):
        for side in range(2):
            for chunk in range(CHUNKS):
                row_copy(step, side, chunk).wait_send()

    def drain(cb, carry):
        store(cb, field).wait()
        return carry

    lax.fori_loop(0, columns, drain, 0)


def on_device(displacement, spring, stiff_table, match_blocks, match_class):
    fields, _, height, breadth = displacement.shape
    columns = breadth // LANES
    matches = match_class.shape[1]
    both = 2 * matches
    width = fields * LANES
    vmem, smem, dma = pltpu.VMEM, pltpu.SMEM, pltpu.SemaphoreType.DMA
    padded = (fields, columns + 2, height + 2 * PAD, LANES)
    anywhere = pl.BlockSpec(memory_space=pl.ANY)
    return pl.pallas_call(
        kernel,
        out_shape=jax.ShapeDtypeStruct(displacement.shape, F32),
        in_specs=[anywhere, anywhere, pl.BlockSpec(memory_space=smem), anywhere, anywhere],
        out_specs=anywhere,
        scratch_shapes=[
            vmem(padded, F32), vmem(padded, F32),
            vmem((columns, height, LANES), F32),
            vmem((columns, height, LANES), F32),
            vmem((columns, height, LANES), F32),
            vmem((columns, height, both), BF16),
            vmem((both, both), BF16),
            smem((1, matches), jnp.int32), smem((1, matches), jnp.int32),
            vmem((1, matches), jnp.int32), vmem((1, matches), jnp.int32),
            vmem((1, matches), jnp.int32), vmem((1, matches), jnp.int32),
            vmem((both, LANES), F32), vmem((both, LANES), F32), vmem((both, LANES), F32),
            vmem((fields, both, LANES), F32),
            vmem((ITERS, fields, both, LANES), F32), vmem((ITERS, fields, both, LANES), F32),
            vmem((both, width), BF16), vmem((both, width), BF16),
            vmem((ITERS, 2, fields * columns, LANES), F32), vmem((ITERS, 2, fields * columns, LANES), F32),
            dma((columns,)), dma((columns,)), dma((3,)), dma((2,)), dma((2,)),
            dma((ITERS, 2, CHUNKS)), dma((ITERS, 2, CHUNKS)), dma((ITERS, 2)), dma((ITERS, 2)),
            dma((columns,)),
        ],
        compiler_params=pltpu.CompilerParams(
            collective_id=0, has_side_effects=True, vmem_limit_bytes=48 * 1024 * 1024
        ),
    )(displacement, spring, stiff_table, match_blocks, match_class)


def solution(mesh):
    placed = (
        P(None, "sec", "tile", None),
        P("sec", "tile", None),
        P(),
        P(None, "sec", "tile"),
        P("sec", "tile"),
    )
    return jax.shard_map(
        on_device,
        mesh=mesh,
        in_specs=placed,
        out_specs=P(None, "sec", "tile", None),
        check_vma=False,
    )
```

```python
import jax
import jax.numpy as jnp
from jax import lax
from jax.experimental import pallas as pl
from jax.experimental.pallas import tpu as pltpu
from jax.sharding import PartitionSpec as P

ITERS = 3
LANES = 128
PAD = 8
CHUNKS = 2
STRIP = 64
MESH = pl.DeviceIdType.MESH
F32 = jnp.float32
BF16 = jnp.bfloat16
I32 = jnp.int32


def split(value):
    high = value.astype(BF16)
    return high, (value - high.astype(F32)).astype(BF16)


def loop(count, body):
    def step(i, carry):
        body(i)
        return carry

    lax.fori_loop(0, count, step, 0)


def relax(
    disp, spring, table_hbm, blocks, classes,
    f_b, last_rows, index,
    f_a, spr, a_ref, g_ref, onehot, pmat,
    table, raw_blocks, lists_out, lists_in, lists_own,
    cmat, c_parts, block_cols, gathered_g, gathered_l, sent, received, terms,
    edge_out, edge_in,
    load_sem, spring_sem, list_sem, list_send, list_recv,
    row_send, row_recv, edge_send, edge_recv,
):
    fields, _, height, breadth = disp.shape
    columns = breadth // LANES
    stride = height + PAD
    matches = classes.shape[1]
    both = 2 * matches
    part = matches // CHUNKS
    section, sections = lax.axis_index("sec"), lax.axis_size("sec")
    tile, tiles = lax.axis_index("tile"), lax.axis_size("tile")
    has_next, has_prev = section < sections - 1, section > 0
    has_upper, has_lower = tile > 0, tile < tiles - 1
    neighbours = (
        (has_next, {"sec": section + 1}),
        (has_prev, {"sec": section - 1}),
        (has_upper, {"tile": tile - 1}),
        (has_lower, {"tile": tile + 1}),
    )

    def first_row(cb):
        return pl.multiple_of((cb + 1) * stride + PAD, PAD)

    def lanes_of(cb):
        return pl.ds(pl.multiple_of(cb * LANES, LANES), LANES)

    barrier = pltpu.get_barrier_semaphore()
    for there, peer in neighbours:

        @pl.when(there)
        def _(peer=peer):
            pl.semaphore_signal(barrier, inc=1, device_id=peer, device_id_type=MESH)

    own_copies = [
        pltpu.make_async_copy(blocks, raw_blocks, list_sem.at[0]),
        pltpu.make_async_copy(classes, lists_own.at[1], list_sem.at[1]),
        pltpu.make_async_copy(table_hbm, table, list_sem.at[2]),
    ]
    for copy in own_copies:
        copy.start()

    def load_field(cb):
        return pltpu.make_async_copy(
            disp.at[:, 0, :, lanes_of(cb)], f_a.at[:, pl.ds(first_row(cb), height), :], load_sem.at[cb]
        )

    def load_spring(cb):
        return pltpu.make_async_copy(spring.at[0, :, lanes_of(cb)], spr.at[cb], spring_sem.at[cb])

    loop(columns, lambda cb: load_field(cb).start())
    loop(columns, lambda cb: load_spring(cb).start())

    zero_block = jnp.zeros((fields, stride, LANES), F32)
    zero_pad = jnp.zeros((fields, PAD, LANES), F32)
    for field in (f_a, f_b):
        field[:, 0:stride, :] = zero_block
        field[:, (columns + 1) * stride + PAD :, :] = zero_block
        loop(columns, lambda cb: field.__setitem__((slice(None), pl.ds(first_row(cb) + height, PAD), slice(None)), zero_pad))
    for there, side in ((has_next, 0), (has_prev, 1)):

        @pl.when(jnp.logical_not(there))
        def _(side=side):
            received[:, :, side * matches : (side + 1) * matches, :] = jnp.zeros((ITERS, fields, matches, LANES), F32)

    for copy in own_copies:
        copy.wait()

    def address(block):
        return (block % columns + 1) * stride + PAD + block // columns

    lists_own[0] = address(raw_blocks[0])
    lists_out[0] = address(raw_blocks[1])
    lists_out[1] = lists_own[1]
    own_scalar = pltpu.make_async_copy(lists_own.at[0], index.at[0], list_sem.at[0])
    own_scalar.start()

    pl.semaphore_wait(barrier, sum(there.astype(I32) for there, _ in neighbours))

    list_copy = pltpu.make_async_remote_copy(
        src_ref=lists_out, dst_ref=lists_in, send_sem=list_send, recv_sem=list_recv,
        device_id={"sec": section + 1}, device_id_type=MESH,
    )
    pl.when(has_next)(list_copy.start)

    def edge_copy(step, way):
        return pltpu.make_async_remote_copy(
            src_ref=edge_out.at[step, way], dst_ref=edge_in.at[step, 1 - way],
            send_sem=edge_send.at[step, way], recv_sem=edge_recv.at[step, 1 - way],
            device_id=neighbours[2 + way][1], device_id_type=MESH,
        )

    def edge_arrival(step, way):
        return pltpu.make_async_remote_copy(
            src_ref=edge_out.at[step, way], dst_ref=edge_in.at[step, way],
            send_sem=edge_send.at[step, way], recv_sem=edge_recv.at[step, way],
            device_id=neighbours[2 + way][1], device_id_type=MESH,
        )

    def row_copy(step, side, chunk, arrival=False):
        mine = side * matches + chunk * part
        theirs = mine if arrival else (1 - side) * matches + chunk * part
        return pltpu.make_async_remote_copy(
            src_ref=sent.at[step, :, pl.ds(mine, part), :],
            dst_ref=received.at[step, :, pl.ds(theirs, part), :],
            send_sem=row_send.at[step, side, chunk],
            recv_sem=row_recv.at[step, side if arrival else 1 - side, chunk],
            device_id=neighbours[side][1], device_id_type=MESH,
        )

    def send_rows(step, side, chunk):
        pl.when(neighbours[side][0])(row_copy(step, side, chunk).start)

    def gather(side, first, count, source, put):
        def group(g):
            at = pl.multiple_of(first + g * 16, 16)
            rows = [source(index[side, 0, at + j]) for j in range(16)]
            for j in range(16):
                put(side * matches + at + j, rows[j])

        loop(count // 16, group)

    def rows_of(ref):
        return lambda at: ref[:, pl.ds(at, 1), :]

    def put_sent(at, row):
        sent[0, :, pl.ds(at, 1), :] = row

    def put_l(at, row):
        gathered_l[:, pl.ds(at, 1), :] = row

    def put_g(at, row):
        gathered_g[pl.ds(at, 1), :] = row

    own_scalar.wait()
    loop(columns, lambda cb: load_field(cb).wait())
    for chunk in range(CHUNKS):
        gather(0, chunk * part, part, rows_of(f_a), put_sent)
        send_rows(0, 0, chunk)

    def send_edges(step, field):
        def one(cb):
            top = first_row(cb)
            for c in range(fields):
                at = pl.ds(c * columns + cb, 1)
                edge_out[step, 0, at, :] = field[c, pl.ds(top, 1), :]
                edge_out[step, 1, at, :] = field[c, pl.ds(top + height - 1, 1), :]

        loop(columns, one)
        for way in range(2):
            pl.when(neighbours[2 + way][0])(edge_copy(step, way).start)

    send_edges(0, f_a)

    def stiffness(lists, alive):
        kind = lists[1]
        stiff = jnp.zeros(kind.shape, F32)
        for level in range(table.shape[0]):
            stiff = jnp.where(kind == level, table[level], stiff)
        return stiff * jnp.where(alive, 1.0, 0.0)

    def fill_side(side, lists, alive):
        half = pl.ds(side * matches, matches)
        wanted = lists[0]
        stiff = jnp.transpose(jnp.broadcast_to(stiffness(lists, alive), (LANES, matches)))
        cmat[half, :] = stiff
        high, low = split(stiff)
        c_parts[half, 0:LANES] = high
        c_parts[half, LANES:] = low
        block_cols[half, :] = jnp.transpose(jnp.broadcast_to(wanted.astype(F32), (LANES, matches)))

        def one(g):
            cb, strip = g // (height // STRIP), g % (height // STRIP)
            row = first_row(cb) + strip * STRIP + lax.broadcasted_iota(I32, (STRIP, LANES), 0)
            at = pl.ds(pl.multiple_of(g * STRIP, STRIP), STRIP)
            for j in range(matches // LANES):
                hit = row == wanted[:, j * LANES : (j + 1) * LANES]
                first = side * matches + j * LANES
                onehot[at, first : first + LANES] = jnp.where(hit, 1.0, 0.0).astype(BF16)

        loop(columns * (height // STRIP), one)

    fill_side(0, lists_own, has_next)

    @pl.when(has_prev)
    def _():
        list_copy.wait_recv()

    @pl.when(jnp.logical_not(has_prev))
    def _():
        lists_in[...] = lists_out[...]

    prev_scalar = pltpu.make_async_copy(lists_in.at[0], index.at[1], list_sem.at[0])
    prev_scalar.start()
    prev_scalar.wait()
    for chunk in range(CHUNKS):
        gather(1, chunk * part, part, rows_of(f_a), put_sent)
        send_rows(0, 1, chunk)
    fill_side(1, lists_in, has_prev)

    def fill_pmat(g):
        at = pl.ds(pl.multiple_of(g * STRIP, STRIP), STRIP)
        col = block_cols[at, :]
        for side, lists in enumerate((lists_own, lists_in)):
            row = lists[0].astype(F32)
            for j in range(matches // LANES):
                hit = jnp.where(col == row[:, j * LANES : (j + 1) * LANES], 1.0, 0.0).astype(BF16)
                first = side * matches + j * LANES
                pmat[at, first : first + LANES] = hit
                pmat[at, both + first : both + first + LANES] = hit

    loop(both // STRIP, fill_pmat)

    def fill_gain(p):
        for q in range(2):
            cb = p * 2 + q
            load_spring(cb).wait()
            at = pl.ds(pl.multiple_of(cb * height, height), height)
            sums = jnp.dot(onehot[at, :], c_parts[...], preferred_element_type=F32)
            stiff = spr[cb]
            gain = 0.8 / (4.0 * stiff + (sums[:, :LANES] + sums[:, LANES:]))
            at = pl.ds(first_row(cb), height)
            g_ref[at, :] = gain
            a_ref[at, :] = gain * stiff

    loop(columns // 2, fill_gain)
    for side in range(2):
        gather(side, 0, matches, lambda at: g_ref[pl.ds(at, 1), :], put_g)

    lane = lax.broadcasted_iota(I32, (STRIP, LANES), 1)

    def stencil(field, result):
        def one(cb):
            for s in range(height // STRIP):
                top = first_row(cb) + s * STRIP
                at = pl.ds(top, STRIP)
                a = a_ref[at, :]
                for c in range(fields):
                    here = field[c, at, :]
                    west, east = field[c, pl.ds(top - stride, STRIP), :], field[c, pl.ds(top + stride, STRIP), :]
                    north, south = field[c, pl.ds(top - 1, STRIP), :], field[c, pl.ds(top + 1, STRIP), :]
                    west = pltpu.roll(jnp.where(lane == LANES - 1, west, here), 1, axis=1)
                    east = pltpu.roll(jnp.where(lane == 0, east, here), LANES - 1, axis=1)
                    result[c, at, :] = here + a * (((north + south) + (west + east)) - 4.0 * here)

        loop(columns, one)

    def add_edges(step, result):
        for way in range(2):

            @pl.when(neighbours[2 + way][0])
            def _(way=way):
                edge_arrival(step, way).wait_recv()

                def one(cb):
                    at = pl.ds(first_row(cb) + way * (height - 1), 1)
                    a = a_ref[at, :]
                    for c in range(fields):
                        result[c, at, :] += a * edge_in[step, way, pl.ds(c * columns + cb, 1), :]

                loop(columns, one)

    group = 4

    def update(g, result):
        at = pl.ds(pl.multiple_of(g * group * height, group * height), group * height)
        sums = jnp.dot(onehot[at, :], terms[0:both, :], preferred_element_type=F32)
        sums = sums + jnp.dot(onehot[at, :], terms[both:, :], preferred_element_type=F32)
        for w in range(group):
            at = pl.ds(first_row(g * group + w), height)
            gain = g_ref[at, :]
            for c in range(fields):
                result[c, at, :] += gain * sums[w * height : (w + 1) * height, c * LANES : (c + 1) * LANES]

    field, result = f_a, f_b
    for step in range(ITERS):
        last = step == ITERS - 1
        stencil(field, result)
        add_edges(step, result)
        for side in range(2):
            gather(side, 0, matches, rows_of(result), put_l)
        for chunk in range(CHUNKS):
            for side in range(2):
                pl.when(neighbours[side][0])(row_copy(step, side, chunk, True).wait_recv)
                first = side * matches + chunk * part
                at = pl.ds(first, part)
                c = cmat[at, :]
                for f in range(fields):
                    lanes = slice(f * LANES, (f + 1) * LANES)
                    high, low = split(c * (received[step, f, at, :] - sent[step, f, at, :]))
                    terms[first : first + part, lanes] = high
                    terms[both + first : both + first + part, lanes] = low
        for chunk in range(CHUNKS):
            for side in range(2):
                at = pl.ds(side * matches + chunk * part, part)
                sums = jnp.dot(pmat[at, :], terms[...], preferred_element_type=F32)
                gain = gathered_g[at, :]
                for f in range(fields):
                    row = gathered_l[f, at, :] + gain * sums[:, f * LANES : (f + 1) * LANES]
                    if last:
                        last_rows[f, at, :] = row
                    else:
                        sent[step + 1, f, at, :] = row
                if not last:
                    send_rows(step + 1, side, chunk)
        if not last:
            loop(columns // group, lambda g: update(g, result))
            send_edges(step + 1, result)
        field, result = result, field

    pl.when(has_next)(list_copy.wait_send)
    for step in range(ITERS):
        for way in range(2):
            pl.when(neighbours[2 + way][0])(edge_copy(step, way).wait_send)
        for side in range(2):
            for chunk in range(CHUNKS):
                pl.when(neighbours[side][0])(row_copy(step, side, chunk).wait_send)


def finish(base, rows, index, out, field, scalar, index_sem, out_sem):
    fields, _, height, breadth = out.shape
    columns = breadth // LANES
    stride = height + PAD
    matches = index.shape[2]

    def group(side):
        def one(g):
            at = pl.multiple_of(g * 16, 16)
            got = [rows[:, pl.ds(side * matches + at + j, 1), :] for j in range(16)]
            for j in range(16):
                field[:, pl.ds(index[side, 0, at + j], 1), :] = got[j]

        return one

    for side in range(2):
        loop(matches // 16, group(side))

    def store(cb):
        top = pl.multiple_of((cb + 1) * stride + PAD, PAD)
        lanes = pl.ds(pl.multiple_of(cb * LANES, LANES), LANES)
        return pltpu.make_async_copy(field.at[:, pl.ds(top, height), :], out.at[:, 0, :, lanes], out_sem.at[cb])

    loop(columns, lambda cb: store(cb).start())
    loop(columns, lambda cb: store(cb).wait())


def on_device(displacement, spring, stiff_table, match_blocks, match_class):
    fields, _, height, breadth = displacement.shape
    columns = breadth // LANES
    matches = match_class.shape[1]
    both = 2 * matches
    width = fields * LANES
    vmem, smem, dma = pltpu.VMEM, pltpu.SMEM, pltpu.SemaphoreType.DMA
    total = (columns + 2) * (height + PAD) + PAD
    padded = (fields, total, LANES)
    anywhere = pl.BlockSpec(memory_space=pl.ANY)
    in_vmem, in_smem = pl.BlockSpec(memory_space=vmem), pl.BlockSpec(memory_space=smem)
    arguments = [
        pltpu.with_memory_space_constraint(x, pltpu.HBM)
        for x in (displacement, spring, stiff_table, match_blocks, match_class)
    ]
    base, rows, index = pl.pallas_call(
        relax,
        out_shape=(vmem(padded, F32), vmem((fields, both, LANES), F32), smem((2, 1, matches), I32)),
        in_specs=[anywhere] * 5,
        out_specs=(in_vmem, in_vmem, in_smem),
        scratch_shapes=[
            vmem(padded, F32),
            vmem((columns, height, LANES), F32),
            vmem((total, LANES), F32), vmem((total, LANES), F32),
            vmem((columns * height, both), BF16),
            vmem((both, 2 * both), BF16),
            smem(stiff_table.shape, F32),
            vmem((2, 1, matches), I32), vmem((2, 1, matches), I32), vmem((2, 1, matches), I32), vmem((2, 1, matches), I32),
            vmem((both, LANES), F32), vmem((both, width), BF16), vmem((both, LANES), F32), vmem((both, LANES), F32),
            vmem((fields, both, LANES), F32),
            vmem((ITERS, fields, both, LANES), F32), vmem((ITERS, fields, both, LANES), F32),
            vmem((2 * both, width), BF16),
            vmem((ITERS, 2, fields * columns, LANES), F32), vmem((ITERS, 2, fields * columns, LANES), F32),
            dma((columns,)), dma((columns,)), dma((3,)), dma, dma,
            dma((ITERS, 2, CHUNKS)), dma((ITERS, 2, CHUNKS)), dma((ITERS, 2)), dma((ITERS, 2)),
        ],
        compiler_params=pltpu.CompilerParams(
            collective_id=0, has_side_effects=True, vmem_limit_bytes=48 * 1024 * 1024
        ),
    )(*arguments)
    relaxed, _ = pl.pallas_call(
        finish,
        out_shape=(jax.ShapeDtypeStruct(displacement.shape, F32), vmem(padded, F32)),
        in_specs=[in_vmem, in_vmem, in_smem],
        out_specs=(anywhere, in_vmem),
        scratch_shapes=[smem((2, 1, matches), I32), dma, dma((columns,))],
        input_output_aliases={0: 1},
        compiler_params=pltpu.CompilerParams(vmem_limit_bytes=24 * 1024 * 1024),
    )(base, rows, index)
    return relaxed


def solution(mesh):
    placed = (
        P(None, "sec", "tile", None),
        P("sec", "tile", None),
        P(),
        P(None, "sec", "tile"),
        P("sec", "tile"),
    )
    return jax.shard_map(
        on_device,
        mesh=mesh,
        in_specs=placed,
        out_specs=P(None, "sec", "tile", None),
        check_vma=False,
    )
```

```python
import jax
import jax.numpy as jnp
from jax import lax
from jax.experimental import pallas as pl
from jax.experimental.pallas import tpu as pltpu
from jax.sharding import PartitionSpec as P

ITERS = 3
LANES = 128
PAD = 8
CHUNKS = 2
LEFT = 2
GROUP = 4
STRIP = 64
MESH = pl.DeviceIdType.MESH
F32 = jnp.float32
BF16 = jnp.bfloat16
I32 = jnp.int32


def split(value):
    high = value.astype(BF16)
    return high, (value - high.astype(F32)).astype(BF16)


def loop(count, body):
    def step(i, carry):
        body(i)
        return carry

    lax.fori_loop(0, count, step, 0)


def relax(
    disp, spring, table_hbm, blocks, classes,
    f_b, last_rows, index,
    f_a, spr, a_ref, g_ref, onehot, pmat,
    table, raw_blocks, lists_out, lists_in, lists_own,
    cmat, c_parts, block_cols, edge_hot, edge_g, partial, gathered_g, gathered_l, sent, received, terms,
    edge_out, edge_in,
    load_sem, spring_sem, list_sem, list_send, list_recv,
    row_send, row_recv, edge_send, edge_recv,
):
    fields, _, height, breadth = disp.shape
    columns = breadth // LANES
    stride = height + PAD
    matches = classes.shape[1]
    both = 2 * matches
    part = matches // CHUNKS
    section, sections = lax.axis_index("sec"), lax.axis_size("sec")
    tile, tiles = lax.axis_index("tile"), lax.axis_size("tile")
    has_next, has_prev = section < sections - 1, section > 0
    has_upper, has_lower = tile > 0, tile < tiles - 1
    neighbours = (
        (has_next, {"sec": section + 1}),
        (has_prev, {"sec": section - 1}),
        (has_upper, {"tile": tile - 1}),
        (has_lower, {"tile": tile + 1}),
    )

    def first_row(cb):
        return pl.multiple_of((cb + LEFT) * stride + PAD, PAD)

    def lanes_of(cb):
        return pl.ds(pl.multiple_of(cb * LANES, LANES), LANES)

    barrier = pltpu.get_barrier_semaphore()
    for there, peer in neighbours:

        @pl.when(there)
        def _(peer=peer):
            pl.semaphore_signal(barrier, inc=1, device_id=peer, device_id_type=MESH)

    own_copies = [
        pltpu.make_async_copy(blocks, raw_blocks, list_sem.at[0]),
        pltpu.make_async_copy(classes, lists_own.at[1], list_sem.at[1]),
        pltpu.make_async_copy(table_hbm, table, list_sem.at[2]),
    ]
    for copy in own_copies:
        copy.start()

    def load_field(cb):
        return pltpu.make_async_copy(
            disp.at[:, 0, :, lanes_of(cb)], f_a.at[:, pl.ds(first_row(cb), height), :], load_sem.at[cb]
        )

    def load_spring(cb):
        return pltpu.make_async_copy(spring.at[0, :, lanes_of(cb)], spr.at[cb], spring_sem.at[cb])

    loop(columns, lambda cb: load_field(cb).start())
    loop(columns, lambda cb: load_spring(cb).start())

    zero_block = jnp.zeros((fields, stride, LANES), F32)
    zero_pad = jnp.zeros((fields, PAD, LANES), F32)
    for field in (f_a, f_b):
        for cb in range(LEFT):
            field[:, cb * stride : (cb + 1) * stride, :] = zero_block
        field[:, (columns + LEFT) * stride + PAD :, :] = zero_block
        field[:, LEFT * stride : LEFT * stride + PAD, :] = zero_pad
        loop(columns, lambda cb: field.__setitem__((slice(None), pl.ds(first_row(cb) + height, PAD), slice(None)), zero_pad))
    for cb in range(LEFT):
        a_ref[cb * stride : (cb + 1) * stride, :] = zero_block[0]
    for there, side in ((has_next, 0), (has_prev, 1)):

        @pl.when(jnp.logical_not(there))
        def _(side=side):
            received[:, :, side * matches : (side + 1) * matches, :] = jnp.zeros((ITERS, fields, matches, LANES), F32)

    for copy in own_copies:
        copy.wait()

    def address(block):
        return (block % columns + LEFT) * stride + PAD + block // columns

    lists_own[0] = address(raw_blocks[0])
    lists_out[0] = address(raw_blocks[1])
    lists_out[1] = lists_own[1]
    own_scalar = pltpu.make_async_copy(lists_own.at[0], index.at[0], list_sem.at[0])
    own_scalar.start()

    pl.semaphore_wait(barrier, sum(there.astype(I32) for there, _ in neighbours))

    list_copy = pltpu.make_async_remote_copy(
        src_ref=lists_out, dst_ref=lists_in, send_sem=list_send, recv_sem=list_recv,
        device_id={"sec": section + 1}, device_id_type=MESH,
    )
    pl.when(has_next)(list_copy.start)

    def edge_copy(step, way):
        return pltpu.make_async_remote_copy(
            src_ref=edge_out.at[step, way], dst_ref=edge_in.at[step, 1 - way],
            send_sem=edge_send.at[step, way], recv_sem=edge_recv.at[step, 1 - way],
            device_id=neighbours[2 + way][1], device_id_type=MESH,
        )

    def edge_arrival(step, way):
        return pltpu.make_async_remote_copy(
            src_ref=edge_out.at[step, way], dst_ref=edge_in.at[step, way],
            send_sem=edge_send.at[step, way], recv_sem=edge_recv.at[step, way],
            device_id=neighbours[2 + way][1], device_id_type=MESH,
        )

    def row_copy(step, side, chunk, arrival=False):
        mine = side * matches + chunk * part
        theirs = mine if arrival else (1 - side) * matches + chunk * part
        return pltpu.make_async_remote_copy(
            src_ref=sent.at[step, :, pl.ds(mine, part), :],
            dst_ref=received.at[step, :, pl.ds(theirs, part), :],
            send_sem=row_send.at[step, side, chunk],
            recv_sem=row_recv.at[step, side if arrival else 1 - side, chunk],
            device_id=neighbours[side][1], device_id_type=MESH,
        )

    def send_rows(step, side, chunk):
        pl.when(neighbours[side][0])(row_copy(step, side, chunk).start)

    def gather(side, first, count, source, put):
        def group(g):
            at = pl.multiple_of(first + g * 16, 16)
            rows = [source(index[side, 0, at + j]) for j in range(16)]
            for j in range(16):
                put(side * matches + at + j, rows[j])

        loop(count // 16, group)

    def rows_of(ref):
        return lambda at: ref[:, pl.ds(at, 1), :]

    def put_sent(at, row):
        sent[0, :, pl.ds(at, 1), :] = row

    def put_l(at, row):
        gathered_l[:, pl.ds(at, 1), :] = row

    def put_g(at, row):
        gathered_g[pl.ds(at, 1), :] = row

    own_scalar.wait()
    loop(columns, lambda cb: load_field(cb).wait())
    for chunk in range(CHUNKS):
        gather(0, chunk * part, part, rows_of(f_a), put_sent)
        send_rows(0, 0, chunk)

    def send_edges(step):
        for way in range(2):
            pl.when(neighbours[2 + way][0])(edge_copy(step, way).start)

    def each_edge(put):
        def one(cb):
            for way in range(2):
                put(way, cb, first_row(cb) + way * (height - 1))

        loop(columns, one)

    def first_edge(way, cb, row):
        for c in range(fields):
            edge_out[0, way, pl.ds(c * columns + cb, 1), :] = f_a[c, pl.ds(row, 1), :]

    each_edge(first_edge)
    send_edges(0)

    def stiffness(lists, alive):
        kind = lists[1]
        stiff = jnp.zeros(kind.shape, F32)
        for level in range(table.shape[0]):
            stiff = jnp.where(kind == level, table[level], stiff)
        return stiff * jnp.where(alive, 1.0, 0.0)

    def place(side, j):
        first = j * LANES // part * 2 * part + side * part + j * LANES % part
        return slice(first, first + LANES)

    def fill_side(side, lists, alive):
        half = pl.ds(side * matches, matches)
        wanted = lists[0]
        stiff = jnp.transpose(jnp.broadcast_to(stiffness(lists, alive), (LANES, matches)))
        cmat[half, :] = stiff
        high, low = split(stiff)
        for j in range(matches // LANES):
            from_rows = slice(j * LANES, (j + 1) * LANES)
            c_parts[place(side, j), 0:LANES] = high[from_rows]
            c_parts[place(side, j), LANES:] = low[from_rows]
        block_cols[half, :] = jnp.transpose(jnp.broadcast_to(wanted.astype(F32), (LANES, matches)))

        def hits(row, j):
            hit = row == wanted[:, j * LANES : (j + 1) * LANES]
            return jnp.where(hit, 1.0, 0.0).astype(BF16)

        def one(cb):
            row = first_row(cb) + lax.broadcasted_iota(I32, (height, LANES), 0)
            at = pl.ds(pl.multiple_of(cb * height, height), height)
            for j in range(matches // LANES):
                onehot[at, place(side, j)] = hits(row, j)

        loop(columns, one)
        order = lax.broadcasted_iota(I32, (2 * columns, LANES), 0)
        row = (order % columns + LEFT) * stride + PAD + order // columns * (height - 1)
        for j in range(matches // LANES):
            edge_hot[:, place(side, j)] = hits(row, j)

    fill_side(0, lists_own, has_next)

    @pl.when(has_prev)
    def _():
        list_copy.wait_recv()

    @pl.when(jnp.logical_not(has_prev))
    def _():
        lists_in[...] = lists_out[...]

    prev_scalar = pltpu.make_async_copy(lists_in.at[0], index.at[1], list_sem.at[0])
    prev_scalar.start()
    prev_scalar.wait()
    for chunk in range(CHUNKS):
        gather(1, chunk * part, part, rows_of(f_a), put_sent)
        send_rows(0, 1, chunk)
    fill_side(1, lists_in, has_prev)

    def fill_pmat(g):
        at = pl.ds(pl.multiple_of(g * STRIP, STRIP), STRIP)
        col = block_cols[at, :]
        for side, lists in enumerate((lists_own, lists_in)):
            row = lists[0].astype(F32)
            for j in range(matches // LANES):
                hit = jnp.where(col == row[:, j * LANES : (j + 1) * LANES], 1.0, 0.0).astype(BF16)
                pmat[at, place(side, j)] = hit

    loop(both // STRIP, fill_pmat)

    def gains(g):
        at = pl.ds(pl.multiple_of(g * GROUP * height, GROUP * height), GROUP * height)
        sums = jnp.dot(onehot[at, :], c_parts[...], preferred_element_type=F32)
        for w in range(GROUP):
            cb = g * GROUP + w
            here = sums[w * height : (w + 1) * height]
            stiff = spr[cb]
            gain = 0.8 / (4.0 * stiff + (here[:, :LANES] + here[:, LANES:]))
            at = pl.ds(first_row(cb), height)
            g_ref[at, :] = gain
            a_ref[at, :] = gain * stiff

    lane = lax.broadcasted_iota(I32, (STRIP, LANES), 1)

    def stencil(cb, field, result):
        for s in range(height // STRIP):
            top = first_row(cb) + s * STRIP
            at = pl.ds(top, STRIP)
            a = a_ref[at, :]
            for c in range(fields):
                here = field[c, at, :]
                west, east = field[c, pl.ds(top - stride, STRIP), :], field[c, pl.ds(top + stride, STRIP), :]
                north, south = field[c, pl.ds(top - 1, STRIP), :], field[c, pl.ds(top + 1, STRIP), :]
                west = pltpu.roll(jnp.where(lane == LANES - 1, west, here), 1, axis=1)
                east = pltpu.roll(jnp.where(lane == 0, east, here), LANES - 1, axis=1)
                result[c, at, :] = here + a * (((north + south) + (west + east)) - 4.0 * here)

    def add_edges(step, result):
        for way in range(2):

            @pl.when(neighbours[2 + way][0])
            def _(way=way):
                edge_arrival(step, way).wait_recv()

                def one(cb):
                    at = pl.ds(first_row(cb) + way * (height - 1), 1)
                    a = a_ref[at, :]
                    for c in range(fields):
                        result[c, at, :] += a * edge_in[step, way, pl.ds(c * columns + cb, 1), :]

                loop(columns, one)

    def update(g, field):
        at = pl.ds(pl.multiple_of(g * GROUP * height, GROUP * height), GROUP * height)
        sums = jnp.dot(onehot[at, :], terms[0:both, :], preferred_element_type=F32)
        sums = sums + jnp.dot(onehot[at, :], terms[both:, :], preferred_element_type=F32)
        for w in range(GROUP):
            at = pl.ds(first_row(g * GROUP + w), height)
            gain = g_ref[at, :]
            for c in range(fields):
                field[c, at, :] += gain * sums[w * height : (w + 1) * height, c * LANES : (c + 1) * LANES]

    groups = columns // GROUP

    def first_pass(g):
        gains(g + 1)
        for w in range(GROUP):
            stencil(g * GROUP + w, f_a, f_b)

    loop(columns, lambda cb: load_spring(cb).wait())
    gains(0)
    loop(groups - 1, first_pass)
    for w in range(GROUP):
        stencil((groups - 1) * GROUP + w, f_a, f_b)
    for side in range(2):
        gather(side, 0, matches, lambda at: g_ref[pl.ds(at, 1), :], put_g)

    def edge_gain(way, cb, row):
        edge_g[pl.ds(way * columns + cb, 1), :] = g_ref[pl.ds(row, 1), :]

    each_edge(edge_gain)

    field, result = f_a, f_b
    for step in range(ITERS):
        last = step == ITERS - 1
        if step > 0:

            def later_pass(g, field=field, result=result):
                update(g + 1, field)
                for w in range(GROUP):
                    stencil(g * GROUP - 1 + w, field, result)

            update(0, field)
            loop(groups - 1, later_pass)
            for w in range(GROUP + 1):
                stencil((groups - 1) * GROUP - 1 + w, field, result)
        add_edges(step, result)
        for side in range(2):
            gather(side, 0, matches, rows_of(result), put_l)
        if not last:

            def edge_base(way, cb, row, step=step, result=result):
                for c in range(fields):
                    edge_out[step + 1, way, pl.ds(c * columns + cb, 1), :] = result[c, pl.ds(row, 1), :]

            each_edge(edge_base)
        for chunk in range(CHUNKS):
            for side in range(2):
                pl.when(neighbours[side][0])(row_copy(step, side, chunk, True).wait_recv)
                at = pl.ds(side * matches + chunk * part, part)
                first = (2 * chunk + side) * part
                c = cmat[at, :]
                for f in range(fields):
                    lanes = slice(f * LANES, (f + 1) * LANES)
                    high, low = split(c * (received[step, f, at, :] - sent[step, f, at, :]))
                    terms[first : first + part, lanes] = high
                    terms[both + first : both + first + part, lanes] = low
            span = slice(2 * chunk * part, 2 * (chunk + 1) * part)
            low_span = slice(both + span.start, both + span.stop)
            for piece in range(CHUNKS):
                for side in range(2):
                    at = pl.ds(side * matches + piece * part, part)
                    sums = jnp.dot(pmat[at, span], terms[span, :], preferred_element_type=F32)
                    sums = sums + jnp.dot(pmat[at, span], terms[low_span, :], preferred_element_type=F32)
                    if chunk > 0:
                        sums = sums + partial[at, :]
                    if chunk < CHUNKS - 1:
                        partial[at, :] = sums
                        continue
                    gain = gathered_g[at, :]
                    for f in range(fields):
                        row = gathered_l[f, at, :] + gain * sums[:, f * LANES : (f + 1) * LANES]
                        if last:
                            last_rows[f, at, :] = row
                        else:
                            sent[step + 1, f, at, :] = row
                    if not last:
                        send_rows(step + 1, side, piece)
        if not last:
            sums = jnp.dot(edge_hot[...], terms[0:both, :], preferred_element_type=F32)
            sums = sums + jnp.dot(edge_hot[...], terms[both:, :], preferred_element_type=F32)
            for way in range(2):
                here = slice(way * columns, (way + 1) * columns)
                gain = edge_g[here, :]
                for c in range(fields):
                    edge_out[step + 1, way, c * columns : (c + 1) * columns, :] += (
                        gain * sums[here, c * LANES : (c + 1) * LANES]
                    )
            send_edges(step + 1)
        field, result = result, field

    pl.when(has_next)(list_copy.wait_send)
    for step in range(ITERS):
        for way in range(2):
            pl.when(neighbours[2 + way][0])(edge_copy(step, way).wait_send)
        for side in range(2):
            for chunk in range(CHUNKS):
                pl.when(neighbours[side][0])(row_copy(step, side, chunk).wait_send)


def finish(base, rows, index, out, field, out_sem):
    fields, _, height, breadth = out.shape
    columns = breadth // LANES
    stride = height + PAD
    matches = index.shape[2]

    def group(side):
        def one(g):
            at = pl.multiple_of(g * 16, 16)
            got = [rows[:, pl.ds(side * matches + at + j, 1), :] for j in range(16)]
            for j in range(16):
                field[:, pl.ds(index[side, 0, at + j], 1), :] = got[j]

        return one

    for side in range(2):
        loop(matches // 16, group(side))

    def store(cb):
        top = pl.multiple_of((cb + LEFT) * stride + PAD, PAD)
        lanes = pl.ds(pl.multiple_of(cb * LANES, LANES), LANES)
        return pltpu.make_async_copy(field.at[:, pl.ds(top, height), :], out.at[:, 0, :, lanes], out_sem.at[cb])

    loop(columns, lambda cb: store(cb).start())
    loop(columns, lambda cb: store(cb).wait())


def on_device(displacement, spring, stiff_table, match_blocks, match_class):
    fields, _, height, breadth = displacement.shape
    columns = breadth // LANES
    matches = match_class.shape[1]
    both = 2 * matches
    width = fields * LANES
    vmem, smem, dma = pltpu.VMEM, pltpu.SMEM, pltpu.SemaphoreType.DMA
    total = (columns + LEFT + 1) * (height + PAD) + PAD
    padded = (fields, total, LANES)
    anywhere = pl.BlockSpec(memory_space=pl.ANY)
    in_vmem, in_smem = pl.BlockSpec(memory_space=vmem), pl.BlockSpec(memory_space=smem)
    arguments = [
        pltpu.with_memory_space_constraint(x, pltpu.HBM)
        for x in (displacement, spring, stiff_table, match_blocks, match_class)
    ]
    base, rows, index = pl.pallas_call(
        relax,
        out_shape=(vmem(padded, F32), vmem((fields, both, LANES), F32), smem((2, 1, matches), I32)),
        in_specs=[anywhere] * 5,
        out_specs=(in_vmem, in_vmem, in_smem),
        scratch_shapes=[
            vmem(padded, F32),
            vmem((columns, height, LANES), F32),
            vmem((total, LANES), F32), vmem((total, LANES), F32),
            vmem((columns * height, both), BF16),
            vmem((both, both), BF16),
            smem(stiff_table.shape, F32),
            vmem((2, 1, matches), I32), vmem((2, 1, matches), I32), vmem((2, 1, matches), I32), vmem((2, 1, matches), I32),
            vmem((both, LANES), F32), vmem((both, width), BF16), vmem((both, LANES), F32),
            vmem((2 * columns, both), BF16), vmem((2 * columns, LANES), F32), vmem((both, width), F32),
            vmem((both, LANES), F32),
            vmem((fields, both, LANES), F32),
            vmem((ITERS, fields, both, LANES), F32), vmem((ITERS, fields, both, LANES), F32),
            vmem((2 * both, width), BF16),
            vmem((ITERS, 2, fields * columns, LANES), F32), vmem((ITERS, 2, fields * columns, LANES), F32),
            dma((columns,)), dma((columns,)), dma((3,)), dma, dma,
            dma((ITERS, 2, CHUNKS)), dma((ITERS, 2, CHUNKS)), dma((ITERS, 2)), dma((ITERS, 2)),
        ],
        compiler_params=pltpu.CompilerParams(
            collective_id=0, has_side_effects=True, vmem_limit_bytes=48 * 1024 * 1024
        ),
    )(*arguments)
    relaxed, _ = pl.pallas_call(
        finish,
        out_shape=(jax.ShapeDtypeStruct(displacement.shape, F32), vmem(padded, F32)),
        in_specs=[in_vmem, in_vmem, in_smem],
        out_specs=(anywhere, in_vmem),
        scratch_shapes=[dma((columns,))],
        input_output_aliases={0: 1},
        compiler_params=pltpu.CompilerParams(vmem_limit_bytes=24 * 1024 * 1024),
    )(base, rows, index)
    return relaxed


def solution(mesh):
    placed = (
        P(None, "sec", "tile", None),
        P("sec", "tile", None),
        P(),
        P(None, "sec", "tile"),
        P("sec", "tile"),
    )
    return jax.shard_map(
        on_device,
        mesh=mesh,
        in_specs=placed,
        out_specs=P(None, "sec", "tile", None),
        check_vma=False,
    )
```

```python
import jax
import jax.numpy as jnp
from jax import lax
from jax.experimental import pallas as pl
from jax.experimental.pallas import tpu as pltpu
from jax.sharding import PartitionSpec as P

ITERS = 3
LANES = 128
PAD = 8
CHUNKS = 2
LEFT = 2
GROUP = 4
STRIP = 64
MESH = pl.DeviceIdType.MESH
F32 = jnp.float32
BF16 = jnp.bfloat16
I32 = jnp.int32


def split(value):
    high = value.astype(BF16)
    return high, (value - high.astype(F32)).astype(BF16)


def loop(count, body):
    def step(i, carry):
        body(i)
        return carry

    lax.fori_loop(0, count, step, 0)


def relax(
    disp, spring, table_hbm, blocks, classes,
    f_b, last_rows, index,
    f_a, spr, a_ref, g_ref, onehot, pmat,
    table, own_raw, prev_raw, lists_in, lists_own,
    cmat, c_parts, block_cols, edge_hot, edge_g, partial, gathered_g, gathered_l, sent, received, terms,
    edge_out, edge_in,
    load_sem, spring_sem, list_sem, list_send, list_recv,
    row_send, row_recv, edge_send, edge_recv, ready,
):
    fields, _, height, breadth = disp.shape
    columns = breadth // LANES
    stride = height + PAD
    matches = classes.shape[1]
    both = 2 * matches
    part = matches // CHUNKS
    section, sections = lax.axis_index("sec"), lax.axis_size("sec")
    tile, tiles = lax.axis_index("tile"), lax.axis_size("tile")
    has_next, has_prev = section < sections - 1, section > 0
    has_upper, has_lower = tile > 0, tile < tiles - 1
    neighbours = (
        (has_next, {"sec": section + 1}),
        (has_prev, {"sec": section - 1}),
        (has_upper, {"tile": tile - 1}),
        (has_lower, {"tile": tile + 1}),
    )

    shift = columns.bit_length() - 1

    def first_row(cb):
        return pl.multiple_of((cb + LEFT) * stride + PAD, PAD)

    def lanes_of(cb):
        return pl.ds(pl.multiple_of(cb * LANES, LANES), LANES)

    def signal(semaphore, peer):
        pl.semaphore_signal(semaphore, inc=1, device_id=peer, device_id_type=MESH)

    early, late = jnp.logical_and(has_lower, tile % 2 == 1), jnp.logical_and(has_upper, tile % 2 == 0)
    barrier = pltpu.get_barrier_semaphore()
    for i, (there, peer) in enumerate(neighbours):
        greets = jnp.logical_and(there, jnp.logical_not(late)) if i == 2 else there
        pl.when(greets)(lambda peer=peer: signal(barrier, peer))

    own_copies = [
        pltpu.make_async_copy(blocks.at[0], own_raw, list_sem.at[0]),
        pltpu.make_async_copy(blocks.at[0], lists_own.at[0], list_sem.at[1]),
        pltpu.make_async_copy(classes, lists_own.at[1], list_sem.at[2]),
        pltpu.make_async_copy(table_hbm, table, list_sem.at[3]),
    ]
    for copy in own_copies:
        copy.start()

    def load_field(cb):
        return pltpu.make_async_copy(
            disp.at[:, 0, :, lanes_of(cb)], f_a.at[:, pl.ds(first_row(cb), height), :], load_sem.at[cb]
        )

    def load_spring(cb):
        return pltpu.make_async_copy(spring.at[0, :, lanes_of(cb)], spr.at[cb], spring_sem.at[cb])

    loop(columns, lambda cb: load_field(cb).start())

    awaited = [there.astype(I32) for there, _ in neighbours]
    pl.semaphore_wait(barrier, sum(awaited) - early.astype(I32))
    list_copies = [
        pltpu.make_async_remote_copy(
            src_ref=src, dst_ref=dst, send_sem=list_send.at[i], recv_sem=list_recv.at[i],
            device_id={"sec": section + 1}, device_id_type=MESH,
        )
        for i, (src, dst) in enumerate(
            ((blocks.at[1], prev_raw), (blocks.at[1], lists_in.at[0]), (classes, lists_in.at[1]))
        )
    ]

    @pl.when(has_next)
    def _():
        for copy in list_copies:
            copy.start()

    pl.when(late)(lambda: signal(ready, neighbours[2][1]))
    loop(columns, lambda cb: load_spring(cb).start())

    zero_block = jnp.zeros((fields, stride, LANES), F32)
    zero_pad = jnp.zeros((fields, PAD, LANES), F32)
    for field in (f_a, f_b):
        for cb in range(LEFT):
            field[:, cb * stride : (cb + 1) * stride, :] = zero_block
        field[:, (columns + LEFT) * stride + PAD :, :] = zero_block
        field[:, LEFT * stride : LEFT * stride + PAD, :] = zero_pad
        loop(columns, lambda cb: field.__setitem__((slice(None), pl.ds(first_row(cb) + height, PAD), slice(None)), zero_pad))
    for cb in range(LEFT):
        a_ref[cb * stride : (cb + 1) * stride, :] = zero_block[0]
    for there, side in ((has_next, 0), (has_prev, 1)):

        @pl.when(jnp.logical_not(there))
        def _(side=side):
            received[:, :, side * matches : (side + 1) * matches, :] = jnp.zeros((ITERS, fields, matches, LANES), F32)

    def address(block):
        return (block % columns + LEFT) * stride + PAD + block // columns

    def edge_copy(step, way):
        return pltpu.make_async_remote_copy(
            src_ref=edge_out.at[step, way], dst_ref=edge_in.at[step, 1 - way],
            send_sem=edge_send.at[step, way], recv_sem=edge_recv.at[step, 1 - way],
            device_id=neighbours[2 + way][1], device_id_type=MESH,
        )

    def edge_arrival(step, way):
        return pltpu.make_async_remote_copy(
            src_ref=edge_out.at[step, way], dst_ref=edge_in.at[step, way],
            send_sem=edge_send.at[step, way], recv_sem=edge_recv.at[step, way],
            device_id=neighbours[2 + way][1], device_id_type=MESH,
        )

    def row_copy(step, side, chunk, arrival=False):
        mine = side * matches + chunk * part
        theirs = mine if arrival else (1 - side) * matches + chunk * part
        return pltpu.make_async_remote_copy(
            src_ref=sent.at[step, :, pl.ds(mine, part), :],
            dst_ref=received.at[step, :, pl.ds(theirs, part), :],
            send_sem=row_send.at[step, side, chunk],
            recv_sem=row_recv.at[step, side if arrival else 1 - side, chunk],
            device_id=neighbours[side][1], device_id_type=MESH,
        )

    def send_rows(step, side, chunk):
        pl.when(neighbours[side][0])(row_copy(step, side, chunk).start)

    def by_block(side, j):
        block = (own_raw, prev_raw)[side][0, j]
        return ((block & (columns - 1)) + LEFT) * stride + PAD + (block >> shift)

    def by_address(side, j):
        return index[side, 0, j]

    def gather(side, first, count, source, put, find=by_address):
        def group(g):
            at = pl.multiple_of(first + g * 16, 16)
            rows = [source(find(side, at + j)) for j in range(16)]
            for j in range(16):
                put(side * matches + at + j, rows[j])

        loop(count // 16, group)

    def rows_of(ref):
        return lambda at: ref[:, pl.ds(at, 1), :]

    def put_sent(at, row):
        sent[0, :, pl.ds(at, 1), :] = row

    def put_l(at, row):
        gathered_l[:, pl.ds(at, 1), :] = row

    def put_g(at, row):
        gathered_g[pl.ds(at, 1), :] = row

    own_copies[0].wait()
    loop(columns, lambda cb: load_field(cb).wait())
    for chunk in range(CHUNKS):
        gather(0, chunk * part, part, rows_of(f_a), put_sent, by_block)
        send_rows(0, 0, chunk)

    def send_edges(step):
        for way in range(2):
            pl.when(neighbours[2 + way][0])(edge_copy(step, way).start)

    def each_edge(put):
        def one(cb):
            for way in range(2):
                put(way, cb, first_row(cb) + way * (height - 1))

        loop(columns, one)

    def first_edge(way, cb, row):
        for c in range(fields):
            edge_out[0, way, pl.ds(c * columns + cb, 1), :] = f_a[c, pl.ds(row, 1), :]

    each_edge(first_edge)
    for copy in own_copies[1:]:
        copy.wait()
    lists_own[0] = address(lists_own[0])
    own_scalar = pltpu.make_async_copy(lists_own.at[0], index.at[0], list_sem.at[0])
    own_scalar.start()

    def stiffness(lists, alive):
        kind = lists[1]
        stiff = jnp.zeros(kind.shape, F32)
        for level in range(table.shape[0]):
            stiff = jnp.where(kind == level, table[level], stiff)
        return stiff * jnp.where(alive, 1.0, 0.0)

    def place(side, j):
        first = j * LANES // part * 2 * part + side * part + j * LANES % part
        return slice(first, first + LANES)

    def fill_side(side, lists, alive):
        half = pl.ds(side * matches, matches)
        wanted = lists[0]
        stiff = jnp.transpose(jnp.broadcast_to(stiffness(lists, alive), (LANES, matches)))
        cmat[half, :] = stiff
        high, low = split(stiff)
        for j in range(matches // LANES):
            from_rows = slice(j * LANES, (j + 1) * LANES)
            c_parts[place(side, j), 0:LANES] = high[from_rows]
            c_parts[place(side, j), LANES:] = low[from_rows]
        block_cols[half, :] = jnp.transpose(jnp.broadcast_to(wanted.astype(F32), (LANES, matches)))

        def hits(row, j):
            hit = row == wanted[:, j * LANES : (j + 1) * LANES]
            return jnp.where(hit, 1.0, 0.0).astype(BF16)

        def one(cb):
            row = first_row(cb) + lax.broadcasted_iota(I32, (height, LANES), 0)
            at = pl.ds(pl.multiple_of(cb * height, height), height)
            for j in range(matches // LANES):
                onehot[at, place(side, j)] = hits(row, j)

        loop(columns, one)
        order = lax.broadcasted_iota(I32, (2 * columns, LANES), 0)
        row = (order % columns + LEFT) * stride + PAD + order // columns * (height - 1)
        for j in range(matches // LANES):
            edge_hot[:, place(side, j)] = hits(row, j)

    fill_side(0, lists_own, has_next)

    @pl.when(has_prev)
    def _():
        list_copies[0].wait_recv()

    @pl.when(jnp.logical_not(has_prev))
    def _():
        copies = [
            pltpu.make_async_copy(src, dst, list_sem.at[1 + i])
            for i, (src, dst) in enumerate(
                ((blocks.at[1], prev_raw), (blocks.at[1], lists_in.at[0]), (classes, lists_in.at[1]))
            )
        ]
        for copy in copies:
            copy.start()
        for copy in copies:
            copy.wait()

    for chunk in range(CHUNKS):
        gather(1, chunk * part, part, rows_of(f_a), put_sent, by_block)
        send_rows(0, 1, chunk)
    pl.when(early)(lambda: pl.semaphore_wait(ready, 1))
    send_edges(0)

    @pl.when(has_prev)
    def _():
        list_copies[1].wait_recv()
        list_copies[2].wait_recv()

    lists_in[0] = address(lists_in[0])
    prev_scalar = pltpu.make_async_copy(lists_in.at[0], index.at[1], list_sem.at[1])
    prev_scalar.start()
    fill_side(1, lists_in, has_prev)

    def fill_pmat(g):
        at = pl.ds(pl.multiple_of(g * STRIP, STRIP), STRIP)
        col = block_cols[at, :]
        for side, lists in enumerate((lists_own, lists_in)):
            row = lists[0].astype(F32)
            for j in range(matches // LANES):
                hit = jnp.where(col == row[:, j * LANES : (j + 1) * LANES], 1.0, 0.0).astype(BF16)
                pmat[at, place(side, j)] = hit

    loop(both // STRIP, fill_pmat)

    def gains(g):
        at = pl.ds(pl.multiple_of(g * GROUP * height, GROUP * height), GROUP * height)
        sums = jnp.dot(onehot[at, :], c_parts[...], preferred_element_type=F32)
        for w in range(GROUP):
            cb = g * GROUP + w
            here = sums[w * height : (w + 1) * height]
            stiff = spr[cb]
            gain = 0.8 / (4.0 * stiff + (here[:, :LANES] + here[:, LANES:]))
            at = pl.ds(first_row(cb), height)
            g_ref[at, :] = gain
            a_ref[at, :] = gain * stiff

    lane = lax.broadcasted_iota(I32, (STRIP, LANES), 1)

    def stencil(cb, field, result):
        for s in range(height // STRIP):
            top = first_row(cb) + s * STRIP
            at = pl.ds(top, STRIP)
            a = a_ref[at, :]
            for c in range(fields):
                here = field[c, at, :]
                west, east = field[c, pl.ds(top - stride, STRIP), :], field[c, pl.ds(top + stride, STRIP), :]
                north, south = field[c, pl.ds(top - 1, STRIP), :], field[c, pl.ds(top + 1, STRIP), :]
                west = pltpu.roll(jnp.where(lane == LANES - 1, west, here), 1, axis=1)
                east = pltpu.roll(jnp.where(lane == 0, east, here), LANES - 1, axis=1)
                result[c, at, :] = here + a * (((north + south) + (west + east)) - 4.0 * here)

    def add_edges(step, result):
        for way in range(2):

            @pl.when(neighbours[2 + way][0])
            def _(way=way):
                edge_arrival(step, way).wait_recv()

                def one(cb):
                    at = pl.ds(first_row(cb) + way * (height - 1), 1)
                    a = a_ref[at, :]
                    for c in range(fields):
                        result[c, at, :] += a * edge_in[step, way, pl.ds(c * columns + cb, 1), :]

                loop(columns, one)

    def update(g, field):
        at = pl.ds(pl.multiple_of(g * GROUP * height, GROUP * height), GROUP * height)
        sums = jnp.dot(onehot[at, :], terms[0:both, :], preferred_element_type=F32)
        sums = sums + jnp.dot(onehot[at, :], terms[both:, :], preferred_element_type=F32)
        for w in range(GROUP):
            at = pl.ds(first_row(g * GROUP + w), height)
            gain = g_ref[at, :]
            for c in range(fields):
                field[c, at, :] += gain * sums[w * height : (w + 1) * height, c * LANES : (c + 1) * LANES]

    groups = columns // GROUP

    def first_pass(g):
        gains(g + 1)
        for w in range(GROUP):
            stencil(g * GROUP + w, f_a, f_b)

    loop(columns, lambda cb: load_spring(cb).wait())
    gains(0)
    loop(groups - 1, first_pass)
    for w in range(GROUP):
        stencil((groups - 1) * GROUP + w, f_a, f_b)
    own_scalar.wait()
    prev_scalar.wait()
    for side in range(2):
        gather(side, 0, matches, lambda at: g_ref[pl.ds(at, 1), :], put_g)

    def edge_gain(way, cb, row):
        edge_g[pl.ds(way * columns + cb, 1), :] = g_ref[pl.ds(row, 1), :]

    each_edge(edge_gain)

    field, result = f_a, f_b
    for step in range(ITERS):
        last = step == ITERS - 1
        if step > 0:

            def later_pass(g, field=field, result=result):
                update(g + 1, field)
                for w in range(GROUP):
                    stencil(g * GROUP - 1 + w, field, result)

            update(0, field)
            loop(groups - 1, later_pass)
            for w in range(GROUP + 1):
                stencil((groups - 1) * GROUP - 1 + w, field, result)
        add_edges(step, result)
        for side in range(2):
            gather(side, 0, matches, rows_of(result), put_l)
        if not last:

            def edge_base(way, cb, row, step=step, result=result):
                for c in range(fields):
                    edge_out[step + 1, way, pl.ds(c * columns + cb, 1), :] = result[c, pl.ds(row, 1), :]

            each_edge(edge_base)
        for chunk in range(CHUNKS):
            for side in range(2):
                pl.when(neighbours[side][0])(row_copy(step, side, chunk, True).wait_recv)
                at = pl.ds(side * matches + chunk * part, part)
                first = (2 * chunk + side) * part
                c = cmat[at, :]
                for f in range(fields):
                    lanes = slice(f * LANES, (f + 1) * LANES)
                    high, low = split(c * (received[step, f, at, :] - sent[step, f, at, :]))
                    terms[first : first + part, lanes] = high
                    terms[both + first : both + first + part, lanes] = low
            span = slice(2 * chunk * part, 2 * (chunk + 1) * part)
            low_span = slice(both + span.start, both + span.stop)
            for piece in range(CHUNKS):
                for side in range(2):
                    at = pl.ds(side * matches + piece * part, part)
                    sums = jnp.dot(pmat[at, span], terms[span, :], preferred_element_type=F32)
                    sums = sums + jnp.dot(pmat[at, span], terms[low_span, :], preferred_element_type=F32)
                    if chunk > 0:
                        sums = sums + partial[at, :]
                    if chunk < CHUNKS - 1:
                        partial[at, :] = sums
                        continue
                    gain = gathered_g[at, :]
                    for f in range(fields):
                        row = gathered_l[f, at, :] + gain * sums[:, f * LANES : (f + 1) * LANES]
                        if last:
                            last_rows[f, at, :] = row
                        else:
                            sent[step + 1, f, at, :] = row
                    if not last:
                        send_rows(step + 1, side, piece)
        if not last:
            sums = jnp.dot(edge_hot[...], terms[0:both, :], preferred_element_type=F32)
            sums = sums + jnp.dot(edge_hot[...], terms[both:, :], preferred_element_type=F32)
            for way in range(2):
                here = slice(way * columns, (way + 1) * columns)
                gain = edge_g[here, :]
                for c in range(fields):
                    edge_out[step + 1, way, c * columns : (c + 1) * columns, :] += (
                        gain * sums[here, c * LANES : (c + 1) * LANES]
                    )
            send_edges(step + 1)
        field, result = result, field

    @pl.when(has_next)
    def _():
        for copy in list_copies:
            copy.wait_send()

    for step in range(ITERS):
        for way in range(2):
            pl.when(neighbours[2 + way][0])(edge_copy(step, way).wait_send)
        for side in range(2):
            for chunk in range(CHUNKS):
                pl.when(neighbours[side][0])(row_copy(step, side, chunk).wait_send)


def finish(base, rows, index, out, field, out_sem):
    fields, _, height, breadth = out.shape
    columns = breadth // LANES
    stride = height + PAD
    matches = index.shape[2]

    def store(c, cb):
        top = pl.multiple_of((cb + LEFT) * stride + PAD, PAD)
        lanes = pl.ds(pl.multiple_of(cb * LANES, LANES), LANES)
        return pltpu.make_async_copy(field.at[c, pl.ds(top, height), :], out.at[c, 0, :, lanes], out_sem.at[c, cb])

    for c in range(fields):
        for side in range(2):

            def group(g, c=c, side=side):
                at = pl.multiple_of(g * 32, 32)
                got = [rows[c, pl.ds(side * matches + at + j, 1), :] for j in range(32)]
                for j in range(32):
                    field[c, pl.ds(index[side, 0, at + j], 1), :] = got[j]

            loop(matches // 32, group)
        loop(columns, lambda cb: store(c, cb).start())
    for c in range(fields):
        loop(columns, lambda cb: store(c, cb).wait())


def on_device(displacement, spring, stiff_table, match_blocks, match_class):
    fields, _, height, breadth = displacement.shape
    columns = breadth // LANES
    matches = match_class.shape[1]
    both = 2 * matches
    width = fields * LANES
    vmem, smem, dma = pltpu.VMEM, pltpu.SMEM, pltpu.SemaphoreType.DMA
    total = (columns + LEFT + 1) * (height + PAD) + PAD
    padded = (fields, total, LANES)
    anywhere = pl.BlockSpec(memory_space=pl.ANY)
    in_vmem, in_smem = pl.BlockSpec(memory_space=vmem), pl.BlockSpec(memory_space=smem)
    arguments = [
        pltpu.with_memory_space_constraint(x, pltpu.HBM)
        for x in (displacement, spring, stiff_table, match_blocks, match_class)
    ]
    base, rows, index = pl.pallas_call(
        relax,
        out_shape=(vmem(padded, F32), vmem((fields, both, LANES), F32), smem((2, 1, matches), I32)),
        in_specs=[anywhere] * 5,
        out_specs=(in_vmem, in_vmem, in_smem),
        scratch_shapes=[
            vmem(padded, F32),
            vmem((columns, height, LANES), F32),
            vmem((total, LANES), F32), vmem((total, LANES), F32),
            vmem((columns * height, both), BF16),
            vmem((both, both), BF16),
            smem(stiff_table.shape, F32),
            smem((1, matches), I32), smem((1, matches), I32), vmem((2, 1, matches), I32), vmem((2, 1, matches), I32),
            vmem((both, LANES), F32), vmem((both, width), BF16), vmem((both, LANES), F32),
            vmem((2 * columns, both), BF16), vmem((2 * columns, LANES), F32), vmem((both, width), F32),
            vmem((both, LANES), F32),
            vmem((fields, both, LANES), F32),
            vmem((ITERS, fields, both, LANES), F32), vmem((ITERS, fields, both, LANES), F32),
            vmem((2 * both, width), BF16),
            vmem((ITERS, 2, fields * columns, LANES), F32), vmem((ITERS, 2, fields * columns, LANES), F32),
            dma((columns,)), dma((columns,)), dma((4,)), dma((3,)), dma((3,)),
            dma((ITERS, 2, CHUNKS)), dma((ITERS, 2, CHUNKS)), dma((ITERS, 2)), dma((ITERS, 2)),
            pltpu.SemaphoreType.REGULAR,
        ],
        compiler_params=pltpu.CompilerParams(
            collective_id=0, has_side_effects=True, vmem_limit_bytes=48 * 1024 * 1024
        ),
    )(*arguments)
    relaxed, _ = pl.pallas_call(
        finish,
        out_shape=(jax.ShapeDtypeStruct(displacement.shape, F32), vmem(padded, F32)),
        in_specs=[in_vmem, in_vmem, in_smem],
        out_specs=(anywhere, in_vmem),
        scratch_shapes=[dma((fields, columns))],
        input_output_aliases={0: 1},
        compiler_params=pltpu.CompilerParams(vmem_limit_bytes=24 * 1024 * 1024),
    )(base, rows, index)
    return relaxed


def solution(mesh):
    placed = (
        P(None, "sec", "tile", None),
        P("sec", "tile", None),
        P(),
        P(None, "sec", "tile"),
        P("sec", "tile"),
    )
    return jax.shard_map(
        on_device,
        mesh=mesh,
        in_specs=placed,
        out_specs=P(None, "sec", "tile", None),
        check_vma=False,
    )
```

```python
import jax
import jax.numpy as jnp
from jax import lax
from jax.experimental import pallas as pl
from jax.experimental.pallas import tpu as pltpu
from jax.sharding import PartitionSpec as P

ITERS = 3
LANES = 128
PAD = 8
CHUNKS = 2
LEFT = 2
GROUP = 4
STRIP = 64
MESH = pl.DeviceIdType.MESH
F32 = jnp.float32
BF16 = jnp.bfloat16
I32 = jnp.int32


def split(value):
    high = value.astype(BF16)
    return high, (value - high.astype(F32)).astype(BF16)


def loop(count, body):
    def step(i, carry):
        body(i)
        return carry

    lax.fori_loop(0, count, step, 0)


def relax(
    disp, spring, table_hbm, blocks, classes,
    f_b, last_rows, index,
    f_a, spr, a_ref, g_ref, onehot, pmat,
    table, own_raw, prev_raw, lists_in, lists_own, places,
    cmat, c_parts, block_cols, far_cols, edge_hot, edge_g, far_pmat, far_g, far_sums, mine, gathered_g, gathered_l, sent, received, terms,
    edge_out, edge_in,
    load_sem, spring_sem, list_sem, list_send, list_recv,
    row_send, row_recv, edge_send, edge_recv, gain_send, gain_recv, ready,
):
    fields, _, height, breadth = disp.shape
    columns = breadth // LANES
    stride = height + PAD
    matches = classes.shape[1]
    both = 2 * matches
    part = matches // CHUNKS
    section, sections = lax.axis_index("sec"), lax.axis_size("sec")
    tile, tiles = lax.axis_index("tile"), lax.axis_size("tile")
    has_next, has_prev = section < sections - 1, section > 0
    has_upper, has_lower = tile > 0, tile < tiles - 1
    neighbours = (
        (has_next, {"sec": section + 1}),
        (has_prev, {"sec": section - 1}),
        (has_upper, {"tile": tile - 1}),
        (has_lower, {"tile": tile + 1}),
    )

    shift = columns.bit_length() - 1

    def first_row(cb):
        return pl.multiple_of((cb + LEFT) * stride + PAD, PAD)

    def lanes_of(cb):
        return pl.ds(pl.multiple_of(cb * LANES, LANES), LANES)

    def signal(semaphore, peer):
        pl.semaphore_signal(semaphore, inc=1, device_id=peer, device_id_type=MESH)

    early, late = jnp.logical_and(has_lower, tile % 2 == 1), jnp.logical_and(has_upper, tile % 2 == 0)
    barrier = pltpu.get_barrier_semaphore()
    for i, (there, peer) in enumerate(neighbours):
        greets = jnp.logical_and(there, jnp.logical_not(late)) if i == 2 else there
        pl.when(greets)(lambda peer=peer: signal(barrier, peer))

    own_copies = [
        pltpu.make_async_copy(blocks.at[0], own_raw, list_sem.at[0]),
        pltpu.make_async_copy(blocks, lists_own.at[0:2], list_sem.at[1]),
        pltpu.make_async_copy(classes, lists_own.at[2], list_sem.at[2]),
        pltpu.make_async_copy(table_hbm, table, list_sem.at[3]),
    ]
    for copy in own_copies:
        copy.start()

    def load_field(cb):
        return pltpu.make_async_copy(
            disp.at[:, 0, :, lanes_of(cb)], f_a.at[:, pl.ds(first_row(cb), height), :], load_sem.at[cb]
        )

    def load_spring(cb):
        return pltpu.make_async_copy(
            spring.at[0, :, lanes_of(cb)], spr.at[pl.ds(first_row(cb), height), :], spring_sem.at[cb]
        )

    loop(columns, lambda cb: load_field(cb).start())

    awaited = [there.astype(I32) for there, _ in neighbours]
    pl.semaphore_wait(barrier, sum(awaited) - early.astype(I32))
    list_copies = [
        pltpu.make_async_remote_copy(
            src_ref=src, dst_ref=dst, send_sem=list_send.at[i], recv_sem=list_recv.at[i],
            device_id={"sec": section + 1}, device_id_type=MESH,
        )
        for i, (src, dst) in enumerate(
            ((blocks.at[1], prev_raw), (blocks, lists_in.at[0:2]), (classes, lists_in.at[2]))
        )
    ]

    @pl.when(has_next)
    def _():
        for copy in list_copies:
            copy.start()

    pl.when(late)(lambda: signal(ready, neighbours[2][1]))
    loop(columns, lambda cb: load_spring(cb).start())

    zero_block = jnp.zeros((fields, stride, LANES), F32)
    zero_pad = jnp.zeros((fields, PAD, LANES), F32)
    for field in (f_a, f_b):
        for cb in range(LEFT):
            field[:, cb * stride : (cb + 1) * stride, :] = zero_block
        field[:, (columns + LEFT) * stride + PAD :, :] = zero_block
        field[:, LEFT * stride : LEFT * stride + PAD, :] = zero_pad
        loop(columns, lambda cb: field.__setitem__((slice(None), pl.ds(first_row(cb) + height, PAD), slice(None)), zero_pad))
    for cb in range(LEFT):
        a_ref[cb * stride : (cb + 1) * stride, :] = zero_block[0]
    for there, side in ((has_next, 0), (has_prev, 1)):

        @pl.when(jnp.logical_not(there))
        def _(side=side):
            received[:, :, side * matches : (side + 1) * matches, :] = jnp.zeros((ITERS, fields, matches, LANES), F32)
            far_g[side * matches : (side + 1) * matches, :] = jnp.zeros((matches, LANES), F32)

    def address(block):
        return (block % columns + LEFT) * stride + PAD + block // columns

    def edge_copy(step, way):
        return pltpu.make_async_remote_copy(
            src_ref=edge_out.at[step, way], dst_ref=edge_in.at[step, 1 - way],
            send_sem=edge_send.at[step, way], recv_sem=edge_recv.at[step, 1 - way],
            device_id=neighbours[2 + way][1], device_id_type=MESH,
        )

    def edge_arrival(step, way):
        return pltpu.make_async_remote_copy(
            src_ref=edge_out.at[step, way], dst_ref=edge_in.at[step, way],
            send_sem=edge_send.at[step, way], recv_sem=edge_recv.at[step, way],
            device_id=neighbours[2 + way][1], device_id_type=MESH,
        )

    def row_copy(step, side, chunk, arrival=False):
        mine = side * matches + chunk * part
        theirs = mine if arrival else (1 - side) * matches + chunk * part
        return pltpu.make_async_remote_copy(
            src_ref=sent.at[step, :, pl.ds(mine, part), :],
            dst_ref=received.at[step, :, pl.ds(theirs, part), :],
            send_sem=row_send.at[step, side, chunk],
            recv_sem=row_recv.at[step, side if arrival else 1 - side, chunk],
            device_id=neighbours[side][1], device_id_type=MESH,
        )

    def send_rows(step, side, chunk):
        pl.when(neighbours[side][0])(row_copy(step, side, chunk).start)

    def by_block(side, j):
        block = (own_raw, prev_raw)[side][0, j]
        return ((block & (columns - 1)) + LEFT) * stride + PAD + (block >> shift)

    def by_address(side, j):
        return index[side, 0, j]

    def gather(side, first, count, source, put, find=by_address):
        def group(g):
            at = pl.multiple_of(first + g * 16, 16)
            rows = [source(find(side, at + j)) for j in range(16)]
            for j in range(16):
                put(side * matches + at + j, rows[j])

        loop(count // 16, group)

    def rows_of(ref):
        return lambda at: ref[:, pl.ds(at, 1), :]

    def put_sent(at, row):
        sent[0, :, pl.ds(at, 1), :] = row

    def put_l(at, row):
        gathered_l[:, pl.ds(at, 1), :] = row

    def put_g(at, row):
        gathered_g[pl.ds(at, 1), :] = row

    own_copies[0].wait()
    loop(columns, lambda cb: load_field(cb).wait())
    for chunk in range(CHUNKS):
        gather(0, chunk * part, part, rows_of(f_a), put_sent, by_block)
        send_rows(0, 0, chunk)

    def send_edges(step):
        for way in range(2):
            pl.when(neighbours[2 + way][0])(edge_copy(step, way).start)

    def each_edge(put):
        def one(cb):
            for way in range(2):
                put(way, cb, first_row(cb) + way * (height - 1))

        loop(columns, one)

    def first_edge(way, cb, row):
        for c in range(fields):
            edge_out[0, way, pl.ds(c * columns + cb, 1), :] = f_a[c, pl.ds(row, 1), :]

    each_edge(first_edge)
    for copy in own_copies[1:]:
        copy.wait()
    places[0] = address(lists_own[0])
    own_scalar = pltpu.make_async_copy(places.at[0], index.at[0], list_sem.at[0])
    own_scalar.start()

    def stiffness(lists, alive):
        kind = lists[2]
        stiff = jnp.zeros(kind.shape, F32)
        for level in range(table.shape[0]):
            stiff = jnp.where(kind == level, table[level], stiff)
        return stiff * jnp.where(alive, 1.0, 0.0)

    def place(side, j):
        first = side * matches + j * LANES
        return slice(first, first + LANES)

    def columns_of(wanted):
        return jnp.transpose(jnp.broadcast_to(wanted.astype(F32), (LANES, matches)))

    def fill_small(side, lists, alive):
        half = pl.ds(side * matches, matches)
        stiff = jnp.transpose(jnp.broadcast_to(stiffness(lists, alive), (LANES, matches)))
        cmat[half, :] = stiff
        high, low = split(stiff)
        for j in range(matches // LANES):
            from_rows = slice(j * LANES, (j + 1) * LANES)
            c_parts[place(side, j), 0:LANES] = high[from_rows]
            c_parts[place(side, j), LANES:] = low[from_rows]
        block_cols[half, :] = columns_of(lists[side])
        far_cols[half, :] = columns_of(lists[1 - side])

    def fill_large(side):
        wanted = places[side]

        def hits(row, j):
            hit = row == wanted[:, j * LANES : (j + 1) * LANES]
            return jnp.where(hit, 1.0, 0.0).astype(BF16)

        def one(cb):
            row = first_row(cb) + lax.broadcasted_iota(I32, (height, LANES), 0)
            at = pl.ds(pl.multiple_of(cb * height, height), height)
            for j in range(matches // LANES):
                onehot[at, place(side, j)] = hits(row, j)

        loop(columns, one)
        order = lax.broadcasted_iota(I32, (2 * columns, LANES), 0)
        row = (order % columns + LEFT) * stride + PAD + order // columns * (height - 1)
        for j in range(matches // LANES):
            edge_hot[:, place(side, j)] = hits(row, j)

    fill_small(0, lists_own, has_next)
    fill_large(0)

    @pl.when(has_prev)
    def _():
        list_copies[0].wait_recv()

    @pl.when(jnp.logical_not(has_prev))
    def _():
        copies = [
            pltpu.make_async_copy(src, dst, list_sem.at[1 + i])
            for i, (src, dst) in enumerate(
                ((blocks.at[1], prev_raw), (blocks, lists_in.at[0:2]), (classes, lists_in.at[2]))
            )
        ]
        for copy in copies:
            copy.start()
        for copy in copies:
            copy.wait()

    for chunk in range(CHUNKS):
        gather(1, chunk * part, part, rows_of(f_a), put_sent, by_block)
        send_rows(0, 1, chunk)
    pl.when(early)(lambda: pl.semaphore_wait(ready, 1))
    send_edges(0)

    @pl.when(has_prev)
    def _():
        list_copies[1].wait_recv()
        list_copies[2].wait_recv()

    places[1] = address(lists_in[1])
    prev_scalar = pltpu.make_async_copy(places.at[1], index.at[1], list_sem.at[1])
    prev_scalar.start()
    fill_small(1, lists_in, has_prev)

    def hits_of(col, row):
        return jnp.where(col == row, 1.0, 0.0).astype(BF16)

    def fill_pmat(g):
        at = pl.ds(pl.multiple_of(g * STRIP, STRIP), STRIP)
        col = block_cols[at, :]
        for side, lists in enumerate((lists_own, lists_in)):
            row = lists[side].astype(F32)
            for j in range(matches // LANES):
                pmat[at, place(side, j)] = hits_of(col, row[:, j * LANES : (j + 1) * LANES])

    def fill_far(g):
        at = pl.ds(pl.multiple_of(g * STRIP, STRIP), STRIP)
        for side, lists in enumerate((lists_own, lists_in)):
            row = lists[1 - side].astype(F32)
            rows = pl.ds(pl.multiple_of(side * matches + g * STRIP, STRIP), STRIP)
            col = far_cols[rows, :]
            for j in range(matches // LANES):
                far_pmat[rows, j * LANES : (j + 1) * LANES] = hits_of(col, row[:, j * LANES : (j + 1) * LANES])

    loop(both // STRIP, fill_pmat)
    loop(columns, lambda cb: load_spring(cb).wait())
    own_scalar.wait()
    prev_scalar.wait()
    for side in range(2):
        gather(side, 0, matches, lambda at: spr[pl.ds(at, 1), :], put_g)
    sums = jnp.dot(pmat[...], c_parts[...], preferred_element_type=F32)
    gathered_g[...] = 0.8 / (4.0 * gathered_g[...] + (sums[:, :LANES] + sums[:, LANES:]))

    def gain_copy(side, arrival=False):
        theirs = side if arrival else 1 - side
        return pltpu.make_async_remote_copy(
            src_ref=gathered_g.at[pl.ds(side * matches, matches), :],
            dst_ref=far_g.at[pl.ds(theirs * matches, matches), :],
            send_sem=gain_send.at[side], recv_sem=gain_recv.at[theirs],
            device_id=neighbours[side][1], device_id_type=MESH,
        )

    for side in range(2):
        pl.when(neighbours[side][0])(gain_copy(side).start)
    fill_large(1)
    loop(matches // STRIP, fill_far)

    def gains(g):
        at = pl.ds(pl.multiple_of(g * GROUP * height, GROUP * height), GROUP * height)
        sums = jnp.dot(onehot[at, :], c_parts[...], preferred_element_type=F32)
        for w in range(GROUP):
            cb = g * GROUP + w
            here = sums[w * height : (w + 1) * height]
            at = pl.ds(first_row(cb), height)
            stiff = spr[at, :]
            gain = 0.8 / (4.0 * stiff + (here[:, :LANES] + here[:, LANES:]))
            g_ref[at, :] = gain
            a_ref[at, :] = gain * stiff

    lane = lax.broadcasted_iota(I32, (STRIP, LANES), 1)

    def stencil(cb, field, result):
        for s in range(height // STRIP):
            top = first_row(cb) + s * STRIP
            at = pl.ds(top, STRIP)
            a = a_ref[at, :]
            for c in range(fields):
                here = field[c, at, :]
                west, east = field[c, pl.ds(top - stride, STRIP), :], field[c, pl.ds(top + stride, STRIP), :]
                north, south = field[c, pl.ds(top - 1, STRIP), :], field[c, pl.ds(top + 1, STRIP), :]
                west = pltpu.roll(jnp.where(lane == LANES - 1, west, here), 1, axis=1)
                east = pltpu.roll(jnp.where(lane == 0, east, here), LANES - 1, axis=1)
                result[c, at, :] = here + a * (((north + south) + (west + east)) - 4.0 * here)

    def add_edges(step, result):
        for way in range(2):

            @pl.when(neighbours[2 + way][0])
            def _(way=way):
                edge_arrival(step, way).wait_recv()

                def one(cb):
                    at = pl.ds(first_row(cb) + way * (height - 1), 1)
                    a = a_ref[at, :]
                    for c in range(fields):
                        result[c, at, :] += a * edge_in[step, way, pl.ds(c * columns + cb, 1), :]

                loop(columns, one)

    def update(g, field):
        at = pl.ds(pl.multiple_of(g * GROUP * height, GROUP * height), GROUP * height)
        sums = jnp.dot(onehot[at, :], terms[0:both, :], preferred_element_type=F32)
        sums = sums + jnp.dot(onehot[at, :], terms[both:, :], preferred_element_type=F32)
        for w in range(GROUP):
            at = pl.ds(first_row(g * GROUP + w), height)
            gain = g_ref[at, :]
            for c in range(fields):
                field[c, at, :] += gain * sums[w * height : (w + 1) * height, c * LANES : (c + 1) * LANES]

    groups = columns // GROUP

    def first_pass(g):
        gains(g + 1)
        for w in range(GROUP):
            stencil(g * GROUP + w, f_a, f_b)

    gains(0)
    loop(groups - 1, first_pass)
    for w in range(GROUP):
        stencil((groups - 1) * GROUP + w, f_a, f_b)
    def edge_gain(way, cb, row):
        edge_g[pl.ds(way * columns + cb, 1), :] = g_ref[pl.ds(row, 1), :]

    each_edge(edge_gain)

    def product(chosen, side):
        first = side * matches
        sums = jnp.dot(chosen, terms[first : first + matches, :], preferred_element_type=F32)
        first = both + first
        return sums + jnp.dot(chosen, terms[first : first + matches, :], preferred_element_type=F32)

    field, result = f_a, f_b
    for step in range(ITERS):
        last = step == ITERS - 1
        if step > 0:

            def later_pass(g, field=field, result=result):
                update(g + 1, field)
                for w in range(GROUP):
                    stencil(g * GROUP - 1 + w, field, result)

            update(0, field)
            loop(groups - 1, later_pass)
            for w in range(GROUP + 1):
                stencil((groups - 1) * GROUP - 1 + w, field, result)
        add_edges(step, result)
        for side in range(2):
            gather(side, 0, matches, rows_of(result), put_l)
        if not last:

            def edge_base(way, cb, row, step=step, result=result):
                for c in range(fields):
                    edge_out[step + 1, way, pl.ds(c * columns + cb, 1), :] = result[c, pl.ds(row, 1), :]

            each_edge(edge_base)
        if step > 0:
            for side in range(2):
                if step == 1:
                    pl.when(neighbours[side][0])(gain_copy(side, True).wait_recv)
                half = pl.ds(side * matches, matches)
                sums = product(far_pmat[half, :], side)
                for f in range(fields):
                    far_sums[f, half, :] = far_g[half, :] * sums[:, f * LANES : (f + 1) * LANES]
        for side in (1, 0):
            for chunk in range(CHUNKS):
                pl.when(neighbours[side][0])(row_copy(step, side, chunk, True).wait_recv)
                first = side * matches + chunk * part
                at = pl.ds(first, part)
                c = cmat[at, :]
                for f in range(fields):
                    lanes = slice(f * LANES, (f + 1) * LANES)
                    there, here = received[step, f, at, :], sent[0, f, at, :] if step == 0 else mine[f, at, :]
                    if step > 0:
                        there = there - far_sums[f, at, :]
                    high, low = split(c * (there - here))
                    terms[first : first + part, lanes] = high
                    terms[both + first : both + first + part, lanes] = low
            across = slice(side * matches, (side + 1) * matches)
            for chunk in range(CHUNKS):
                at = pl.ds((1 - side) * matches + chunk * part, part)
                sums = product(pmat[at, across], side)
                gain = gathered_g[at, :]
                for f in range(fields):
                    row = gathered_l[f, at, :] + gain * sums[:, f * LANES : (f + 1) * LANES]
                    if last:
                        last_rows[f, at, :] = row
                    else:
                        sent[step + 1, f, at, :] = row
                if not last:
                    send_rows(step + 1, 1 - side, chunk)
        if not last:
            sums = jnp.dot(edge_hot[...], terms[0:both, :], preferred_element_type=F32)
            sums = sums + jnp.dot(edge_hot[...], terms[both:, :], preferred_element_type=F32)
            for way in range(2):
                here = slice(way * columns, (way + 1) * columns)
                gain = edge_g[here, :]
                for c in range(fields):
                    edge_out[step + 1, way, c * columns : (c + 1) * columns, :] += (
                        gain * sums[here, c * LANES : (c + 1) * LANES]
                    )
            send_edges(step + 1)
        for side in range(2):
            half = slice(side * matches, (side + 1) * matches)
            sums = product(pmat[half, half], side)
            gain = gathered_g[half, :]
            for f in range(fields):
                add = gain * sums[:, f * LANES : (f + 1) * LANES]
                if last:
                    last_rows[f, half, :] += add
                else:
                    mine[f, half, :] = sent[step + 1, f, half, :] + add
        field, result = result, field

    @pl.when(has_next)
    def _():
        for copy in list_copies:
            copy.wait_send()

    for side in range(2):
        pl.when(neighbours[side][0])(gain_copy(side).wait_send)
    for step in range(ITERS):
        for way in range(2):
            pl.when(neighbours[2 + way][0])(edge_copy(step, way).wait_send)
        for side in range(2):
            for chunk in range(CHUNKS):
                pl.when(neighbours[side][0])(row_copy(step, side, chunk).wait_send)


def finish(base, rows, index, out, field, out_sem):
    fields, _, height, breadth = out.shape
    columns = breadth // LANES
    stride = height + PAD
    matches = index.shape[2]

    def group(side):
        def one(g):
            at = pl.multiple_of(g * 16, 16)
            got = [rows[:, pl.ds(side * matches + at + j, 1), :] for j in range(16)]
            for j in range(16):
                field[:, pl.ds(index[side, 0, at + j], 1), :] = got[j]

        return one

    for side in range(2):
        loop(matches // 16, group(side))

    def store(cb):
        top = pl.multiple_of((cb + LEFT) * stride + PAD, PAD)
        lanes = pl.ds(pl.multiple_of(cb * LANES, LANES), LANES)
        return pltpu.make_async_copy(field.at[:, pl.ds(top, height), :], out.at[:, 0, :, lanes], out_sem.at[cb])

    loop(columns, lambda cb: store(cb).start())
    loop(columns, lambda cb: store(cb).wait())


def on_device(displacement, spring, stiff_table, match_blocks, match_class):
    fields, _, height, breadth = displacement.shape
    columns = breadth // LANES
    matches = match_class.shape[1]
    both = 2 * matches
    width = fields * LANES
    vmem, smem, dma = pltpu.VMEM, pltpu.SMEM, pltpu.SemaphoreType.DMA
    total = (columns + LEFT + 1) * (height + PAD) + PAD
    padded = (fields, total, LANES)
    anywhere = pl.BlockSpec(memory_space=pl.ANY)
    in_vmem, in_smem = pl.BlockSpec(memory_space=vmem), pl.BlockSpec(memory_space=smem)
    arguments = [
        pltpu.with_memory_space_constraint(x, pltpu.HBM)
        for x in (displacement, spring, stiff_table, match_blocks, match_class)
    ]
    base, rows, index = pl.pallas_call(
        relax,
        out_shape=(vmem(padded, F32), vmem((fields, both, LANES), F32), smem((2, 1, matches), I32)),
        in_specs=[anywhere] * 5,
        out_specs=(in_vmem, in_vmem, in_smem),
        scratch_shapes=[
            vmem(padded, F32),
            vmem((total, LANES), F32), vmem((total, LANES), F32), vmem((total, LANES), F32),
            vmem((columns * height, both), BF16),
            vmem((both, both), BF16),
            smem(stiff_table.shape, F32),
            smem((1, matches), I32), smem((1, matches), I32), vmem((3, 1, matches), I32), vmem((3, 1, matches), I32), vmem((2, 1, matches), I32),
            vmem((both, LANES), F32), vmem((both, width), BF16), vmem((both, LANES), F32), vmem((both, LANES), F32),
            vmem((2 * columns, both), BF16), vmem((2 * columns, LANES), F32), vmem((both, matches), BF16),
            vmem((both, LANES), F32), vmem((fields, both, LANES), F32), vmem((fields, both, LANES), F32),
            vmem((both, LANES), F32),
            vmem((fields, both, LANES), F32),
            vmem((ITERS, fields, both, LANES), F32), vmem((ITERS, fields, both, LANES), F32),
            vmem((2 * both, width), BF16),
            vmem((ITERS, 2, fields * columns, LANES), F32), vmem((ITERS, 2, fields * columns, LANES), F32),
            dma((columns,)), dma((columns,)), dma((4,)), dma((3,)), dma((3,)),
            dma((ITERS, 2, CHUNKS)), dma((ITERS, 2, CHUNKS)), dma((ITERS, 2)), dma((ITERS, 2)), dma((2,)), dma((2,)),
            pltpu.SemaphoreType.REGULAR,
        ],
        compiler_params=pltpu.CompilerParams(
            collective_id=0, has_side_effects=True, vmem_limit_bytes=48 * 1024 * 1024
        ),
    )(*arguments)
    relaxed, _ = pl.pallas_call(
        finish,
        out_shape=(jax.ShapeDtypeStruct(displacement.shape, F32), vmem(padded, F32)),
        in_specs=[in_vmem, in_vmem, in_smem],
        out_specs=(anywhere, in_vmem),
        scratch_shapes=[dma((columns,))],
        input_output_aliases={0: 1},
        compiler_params=pltpu.CompilerParams(vmem_limit_bytes=24 * 1024 * 1024),
    )(base, rows, index)
    return relaxed


def solution(mesh):
    placed = (
        P(None, "sec", "tile", None),
        P("sec", "tile", None),
        P(),
        P(None, "sec", "tile"),
        P("sec", "tile"),
    )
    return jax.shard_map(
        on_device,
        mesh=mesh,
        in_specs=placed,
        out_specs=P(None, "sec", "tile", None),
        check_vma=False,
    )
```

```python
import jax
import jax.numpy as jnp
from jax import lax
from jax.experimental import pallas as pl
from jax.experimental.pallas import tpu as pltpu
from jax.sharding import PartitionSpec as P

ITERS = 3
LANES = 128
PAD = 8
CHUNKS = 2
LEFT = 2
GROUP = 4
STRIP = 64
MESH = pl.DeviceIdType.MESH
F32 = jnp.float32
BF16 = jnp.bfloat16
I32 = jnp.int32


def split(value):
    high = value.astype(BF16)
    return high, (value - high.astype(F32)).astype(BF16)


def loop(count, body):
    def step(i, carry):
        body(i)
        return carry

    lax.fori_loop(0, count, step, 0)


def relax(
    disp, spring, table_hbm, blocks, classes,
    f_b, last_rows, index,
    f_a, spr, a_ref, g_ref, onehot, pmat,
    table, own_raw, prev_raw, lists_in, lists_own,
    cmat, c_parts, block_cols, edge_hot, edge_g, partial, gathered_g, gathered_l, sent, received, terms,
    edge_out, edge_in,
    load_sem, spring_sem, list_sem, list_send, list_recv,
    row_send, row_recv, edge_send, edge_recv, ready,
):
    fields, _, height, breadth = disp.shape
    columns = breadth // LANES
    stride = height + PAD
    matches = classes.shape[1]
    both = 2 * matches
    part = matches // CHUNKS
    section, sections = lax.axis_index("sec"), lax.axis_size("sec")
    tile, tiles = lax.axis_index("tile"), lax.axis_size("tile")
    has_next, has_prev = section < sections - 1, section > 0
    has_upper, has_lower = tile > 0, tile < tiles - 1
    neighbours = (
        (has_next, {"sec": section + 1}),
        (has_prev, {"sec": section - 1}),
        (has_upper, {"tile": tile - 1}),
        (has_lower, {"tile": tile + 1}),
    )

    shift = columns.bit_length() - 1

    def first_row(cb):
        return pl.multiple_of((cb + LEFT) * stride + PAD, PAD)

    def lanes_of(cb):
        return pl.ds(pl.multiple_of(cb * LANES, LANES), LANES)

    def signal(semaphore, peer):
        pl.semaphore_signal(semaphore, inc=1, device_id=peer, device_id_type=MESH)

    early, late = jnp.logical_and(has_lower, tile % 2 == 1), jnp.logical_and(has_upper, tile % 2 == 0)
    barrier = pltpu.get_barrier_semaphore()
    for i, (there, peer) in enumerate(neighbours):
        greets = jnp.logical_and(there, jnp.logical_not(late)) if i == 2 else there
        pl.when(greets)(lambda peer=peer: signal(barrier, peer))

    own_copies = [
        pltpu.make_async_copy(blocks.at[0], own_raw, list_sem.at[0]),
        pltpu.make_async_copy(blocks.at[0], lists_own.at[0], list_sem.at[1]),
        pltpu.make_async_copy(classes, lists_own.at[1], list_sem.at[2]),
        pltpu.make_async_copy(table_hbm, table, list_sem.at[3]),
    ]
    def load_field(cb):
        return pltpu.make_async_copy(
            disp.at[:, 0, :, lanes_of(cb)], f_a.at[:, pl.ds(first_row(cb), height), :], load_sem.at[cb]
        )

    def load_spring(cb):
        return pltpu.make_async_copy(spring.at[0, :, lanes_of(cb)], spr.at[cb], spring_sem.at[cb])


    awaited = [there.astype(I32) for there, _ in neighbours]
    pl.semaphore_wait(barrier, sum(awaited) - early.astype(I32))
    list_copies = [
        pltpu.make_async_remote_copy(
            src_ref=src, dst_ref=dst, send_sem=list_send.at[i], recv_sem=list_recv.at[i],
            device_id={"sec": section + 1}, device_id_type=MESH,
        )
        for i, (src, dst) in enumerate(
            ((blocks.at[1], prev_raw), (blocks.at[1], lists_in.at[0]), (classes, lists_in.at[1]))
        )
    ]

    @pl.when(has_next)
    def _():
        for copy in list_copies:
            copy.start()

    pl.when(late)(lambda: signal(ready, neighbours[2][1]))
    for copy in own_copies:
        copy.start()
    loop(columns, lambda cb: load_field(cb).start())
    loop(columns, lambda cb: load_spring(cb).start())

    zero_block = jnp.zeros((fields, stride, LANES), F32)
    zero_pad = jnp.zeros((fields, PAD, LANES), F32)
    for field in (f_a, f_b):
        for cb in range(LEFT):
            field[:, cb * stride : (cb + 1) * stride, :] = zero_block
        field[:, (columns + LEFT) * stride + PAD :, :] = zero_block
        field[:, LEFT * stride : LEFT * stride + PAD, :] = zero_pad
        loop(columns, lambda cb: field.__setitem__((slice(None), pl.ds(first_row(cb) + height, PAD), slice(None)), zero_pad))
    for cb in range(LEFT):
        a_ref[cb * stride : (cb + 1) * stride, :] = zero_block[0]
    for there, side in ((has_next, 0), (has_prev, 1)):

        @pl.when(jnp.logical_not(there))
        def _(side=side):
            received[:, :, side * matches : (side + 1) * matches, :] = jnp.zeros((ITERS, fields, matches, LANES), F32)

    def address(block):
        return (block % columns + LEFT) * stride + PAD + block // columns

    def edge_copy(step, way):
        return pltpu.make_async_remote_copy(
            src_ref=edge_out.at[step, way], dst_ref=edge_in.at[step, 1 - way],
            send_sem=edge_send.at[step, way], recv_sem=edge_recv.at[step, 1 - way],
            device_id=neighbours[2 + way][1], device_id_type=MESH,
        )

    def edge_arrival(step, way):
        return pltpu.make_async_remote_copy(
            src_ref=edge_out.at[step, way], dst_ref=edge_in.at[step, way],
            send_sem=edge_send.at[step, way], recv_sem=edge_recv.at[step, way],
            device_id=neighbours[2 + way][1], device_id_type=MESH,
        )

    def row_copy(step, side, chunk, arrival=False):
        mine = side * matches + chunk * part
        theirs = mine if arrival else (1 - side) * matches + chunk * part
        return pltpu.make_async_remote_copy(
            src_ref=sent.at[step, :, pl.ds(mine, part), :],
            dst_ref=received.at[step, :, pl.ds(theirs, part), :],
            send_sem=row_send.at[step, side, chunk],
            recv_sem=row_recv.at[step, side if arrival else 1 - side, chunk],
            device_id=neighbours[side][1], device_id_type=MESH,
        )

    def send_rows(step, side, chunk):
        pl.when(neighbours[side][0])(row_copy(step, side, chunk).start)

    def by_block(side, j):
        block = (own_raw, prev_raw)[side][0, j]
        return ((block & (columns - 1)) + LEFT) * stride + PAD + (block >> shift)

    def by_address(side, j):
        return index[side, 0, j]

    def gather(side, first, count, source, put, find=by_address):
        def group(g):
            at = pl.multiple_of(first + g * 16, 16)
            rows = [source(find(side, at + j)) for j in range(16)]
            for j in range(16):
                put(side * matches + at + j, rows[j])

        loop(count // 16, group)

    def rows_of(ref):
        return lambda at: ref[:, pl.ds(at, 1), :]

    def put_sent(at, row):
        sent[0, :, pl.ds(at, 1), :] = row

    def put_l(at, row):
        gathered_l[:, pl.ds(at, 1), :] = row

    def put_g(at, row):
        gathered_g[pl.ds(at, 1), :] = row

    own_copies[0].wait()
    loop(columns, lambda cb: load_field(cb).wait())
    for chunk in range(CHUNKS):
        gather(0, chunk * part, part, rows_of(f_a), put_sent, by_block)
        send_rows(0, 0, chunk)

    def send_edges(step):
        for way in range(2):
            pl.when(neighbours[2 + way][0])(edge_copy(step, way).start)

    def each_edge(put):
        def one(cb):
            for way in range(2):
                put(way, cb, first_row(cb) + way * (height - 1))

        loop(columns, one)

    def first_edge(way, cb, row):
        for c in range(fields):
            edge_out[0, way, pl.ds(c * columns + cb, 1), :] = f_a[c, pl.ds(row, 1), :]

    each_edge(first_edge)
    for copy in own_copies[1:]:
        copy.wait()
    lists_own[0] = address(lists_own[0])
    own_scalar = pltpu.make_async_copy(lists_own.at[0], index.at[0], list_sem.at[0])
    own_scalar.start()

    def stiffness(lists, alive):
        kind = lists[1]
        stiff = jnp.zeros(kind.shape, F32)
        for level in range(table.shape[0]):
            stiff = jnp.where(kind == level, table[level], stiff)
        return stiff * jnp.where(alive, 1.0, 0.0)

    def place(side, j):
        first = j * LANES // part * 2 * part + side * part + j * LANES % part
        return slice(first, first + LANES)

    def fill_side(side, lists, alive):
        half = pl.ds(side * matches, matches)
        wanted = lists[0]
        stiff = jnp.transpose(jnp.broadcast_to(stiffness(lists, alive), (LANES, matches)))
        cmat[half, :] = stiff
        high, low = split(stiff)
        for j in range(matches // LANES):
            from_rows = slice(j * LANES, (j + 1) * LANES)
            c_parts[place(side, j), 0:LANES] = high[from_rows]
            c_parts[place(side, j), LANES:] = low[from_rows]
        block_cols[half, :] = jnp.transpose(jnp.broadcast_to(wanted.astype(F32), (LANES, matches)))

        def hits(row, j):
            hit = row == wanted[:, j * LANES : (j + 1) * LANES]
            return jnp.where(hit, 1.0, 0.0).astype(BF16)

        def one(cb):
            row = first_row(cb) + lax.broadcasted_iota(I32, (height, LANES), 0)
            at = pl.ds(pl.multiple_of(cb * height, height), height)
            for j in range(matches // LANES):
                onehot[at, place(side, j)] = hits(row, j)

        loop(columns, one)
        order = lax.broadcasted_iota(I32, (2 * columns, LANES), 0)
        row = (order % columns + LEFT) * stride + PAD + order // columns * (height - 1)
        for j in range(matches // LANES):
            edge_hot[:, place(side, j)] = hits(row, j)

    fill_side(0, lists_own, has_next)

    @pl.when(has_prev)
    def _():
        list_copies[0].wait_recv()

    @pl.when(jnp.logical_not(has_prev))
    def _():
        copies = [
            pltpu.make_async_copy(src, dst, list_sem.at[1 + i])
            for i, (src, dst) in enumerate(
                ((blocks.at[1], prev_raw), (blocks.at[1], lists_in.at[0]), (classes, lists_in.at[1]))
            )
        ]
        for copy in copies:
            copy.start()
        for copy in copies:
            copy.wait()

    for chunk in range(CHUNKS):
        gather(1, chunk * part, part, rows_of(f_a), put_sent, by_block)
        send_rows(0, 1, chunk)
    pl.when(early)(lambda: pl.semaphore_wait(ready, 1))
    send_edges(0)

    @pl.when(has_prev)
    def _():
        list_copies[1].wait_recv()
        list_copies[2].wait_recv()

    lists_in[0] = address(lists_in[0])
    prev_scalar = pltpu.make_async_copy(lists_in.at[0], index.at[1], list_sem.at[1])
    prev_scalar.start()
    fill_side(1, lists_in, has_prev)

    def fill_pmat(g):
        at = pl.ds(pl.multiple_of(g * STRIP, STRIP), STRIP)
        col = block_cols[at, :]
        for side, lists in enumerate((lists_own, lists_in)):
            row = lists[0].astype(F32)
            for j in range(matches // LANES):
                hit = jnp.where(col == row[:, j * LANES : (j + 1) * LANES], 1.0, 0.0).astype(BF16)
                pmat[at, place(side, j)] = hit

    loop(both // STRIP, fill_pmat)

    def gains(g):
        at = pl.ds(pl.multiple_of(g * GROUP * height, GROUP * height), GROUP * height)
        sums = jnp.dot(onehot[at, :], c_parts[...], preferred_element_type=F32)
        for w in range(GROUP):
            cb = g * GROUP + w
            here = sums[w * height : (w + 1) * height]
            stiff = spr[cb]
            gain = 0.8 / (4.0 * stiff + (here[:, :LANES] + here[:, LANES:]))
            at = pl.ds(first_row(cb), height)
            g_ref[at, :] = gain
            a_ref[at, :] = gain * stiff

    lane = lax.broadcasted_iota(I32, (STRIP, LANES), 1)

    def stencil(cb, field, result):
        for s in range(height // STRIP):
            top = first_row(cb) + s * STRIP
            at = pl.ds(top, STRIP)
            a = a_ref[at, :]
            for c in range(fields):
                here = field[c, at, :]
                west, east = field[c, pl.ds(top - stride, STRIP), :], field[c, pl.ds(top + stride, STRIP), :]
                north, south = field[c, pl.ds(top - 1, STRIP), :], field[c, pl.ds(top + 1, STRIP), :]
                west = pltpu.roll(jnp.where(lane == LANES - 1, west, here), 1, axis=1)
                east = pltpu.roll(jnp.where(lane == 0, east, here), LANES - 1, axis=1)
                result[c, at, :] = here + a * (((north + south) + (west + east)) - 4.0 * here)

    def add_edges(step, result):
        for way in range(2):

            @pl.when(neighbours[2 + way][0])
            def _(way=way):
                edge_arrival(step, way).wait_recv()

                def one(cb):
                    at = pl.ds(first_row(cb) + way * (height - 1), 1)
                    a = a_ref[at, :]
                    for c in range(fields):
                        result[c, at, :] += a * edge_in[step, way, pl.ds(c * columns + cb, 1), :]

                loop(columns, one)

    def update(g, field):
        at = pl.ds(pl.multiple_of(g * GROUP * height, GROUP * height), GROUP * height)
        sums = jnp.dot(onehot[at, :], terms[0:both, :], preferred_element_type=F32)
        sums = sums + jnp.dot(onehot[at, :], terms[both:, :], preferred_element_type=F32)
        for w in range(GROUP):
            at = pl.ds(first_row(g * GROUP + w), height)
            gain = g_ref[at, :]
            for c in range(fields):
                field[c, at, :] += gain * sums[w * height : (w + 1) * height, c * LANES : (c + 1) * LANES]

    groups = columns // GROUP

    def first_pass(g):
        gains(g + 1)
        for w in range(GROUP):
            stencil(g * GROUP + w, f_a, f_b)

    loop(columns, lambda cb: load_spring(cb).wait())
    gains(0)
    loop(groups - 1, first_pass)
    for w in range(GROUP):
        stencil((groups - 1) * GROUP + w, f_a, f_b)
    own_scalar.wait()
    prev_scalar.wait()
    for side in range(2):
        gather(side, 0, matches, lambda at: g_ref[pl.ds(at, 1), :], put_g)

    def edge_gain(way, cb, row):
        edge_g[pl.ds(way * columns + cb, 1), :] = g_ref[pl.ds(row, 1), :]

    each_edge(edge_gain)

    field, result = f_a, f_b
    for step in range(ITERS):
        last = step == ITERS - 1
        if step > 0:

            def later_pass(g, field=field, result=result):
                update(g + 1, field)
                for w in range(GROUP):
                    stencil(g * GROUP - 1 + w, field, result)

            update(0, field)
            loop(groups - 1, later_pass)
            for w in range(GROUP + 1):
                stencil((groups - 1) * GROUP - 1 + w, field, result)
        add_edges(step, result)
        for side in range(2):
            gather(side, 0, matches, rows_of(result), put_l)
        if not last:

            def edge_base(way, cb, row, step=step, result=result):
                for c in range(fields):
                    edge_out[step + 1, way, pl.ds(c * columns + cb, 1), :] = result[c, pl.ds(row, 1), :]

            each_edge(edge_base)
        for chunk in range(CHUNKS):
            for side in range(2):
                pl.when(neighbours[side][0])(row_copy(step, side, chunk, True).wait_recv)
                at = pl.ds(side * matches + chunk * part, part)
                first = (2 * chunk + side) * part
                c = cmat[at, :]
                for f in range(fields):
                    lanes = slice(f * LANES, (f + 1) * LANES)
                    high, low = split(c * (received[step, f, at, :] - sent[step, f, at, :]))
                    terms[first : first + part, lanes] = high
                    terms[both + first : both + first + part, lanes] = low
            span = slice(2 * chunk * part, 2 * (chunk + 1) * part)
            low_span = slice(both + span.start, both + span.stop)
            for piece in range(CHUNKS):
                for side in range(2):
                    at = pl.ds(side * matches + piece * part, part)
                    sums = jnp.dot(pmat[at, span], terms[span, :], preferred_element_type=F32)
                    sums = sums + jnp.dot(pmat[at, span], terms[low_span, :], preferred_element_type=F32)
                    if chunk > 0:
                        sums = sums + partial[at, :]
                    if chunk < CHUNKS - 1:
                        partial[at, :] = sums
                        continue
                    gain = gathered_g[at, :]
                    for f in range(fields):
                        row = gathered_l[f, at, :] + gain * sums[:, f * LANES : (f + 1) * LANES]
                        if last:
                            last_rows[f, at, :] = row
                        else:
                            sent[step + 1, f, at, :] = row
                    if not last:
                        send_rows(step + 1, side, piece)
        if not last:
            sums = jnp.dot(edge_hot[...], terms[0:both, :], preferred_element_type=F32)
            sums = sums + jnp.dot(edge_hot[...], terms[both:, :], preferred_element_type=F32)
            for way in range(2):
                here = slice(way * columns, (way + 1) * columns)
                gain = edge_g[here, :]
                for c in range(fields):
                    edge_out[step + 1, way, c * columns : (c + 1) * columns, :] += (
                        gain * sums[here, c * LANES : (c + 1) * LANES]
                    )
            send_edges(step + 1)
        field, result = result, field

    @pl.when(has_next)
    def _():
        for copy in list_copies:
            copy.wait_send()

    for step in range(ITERS):
        for way in range(2):
            pl.when(neighbours[2 + way][0])(edge_copy(step, way).wait_send)
        for side in range(2):
            for chunk in range(CHUNKS):
                pl.when(neighbours[side][0])(row_copy(step, side, chunk).wait_send)


def finish(base, rows, index, out, field, out_sem):
    fields, _, height, breadth = out.shape
    columns = breadth // LANES
    stride = height + PAD
    matches = index.shape[2]

    def group(side):
        def one(g):
            at = pl.multiple_of(g * 16, 16)
            got = [rows[:, pl.ds(side * matches + at + j, 1), :] for j in range(16)]
            for j in range(16):
                field[:, pl.ds(index[side, 0, at + j], 1), :] = got[j]

        return one

    for side in range(2):
        loop(matches // 16, group(side))

    def store(cb):
        top = pl.multiple_of((cb + LEFT) * stride + PAD, PAD)
        lanes = pl.ds(pl.multiple_of(cb * LANES, LANES), LANES)
        return pltpu.make_async_copy(field.at[:, pl.ds(top, height), :], out.at[:, 0, :, lanes], out_sem.at[cb])

    loop(columns, lambda cb: store(cb).start())
    loop(columns, lambda cb: store(cb).wait())


def on_device(displacement, spring, stiff_table, match_blocks, match_class):
    fields, _, height, breadth = displacement.shape
    columns = breadth // LANES
    matches = match_class.shape[1]
    both = 2 * matches
    width = fields * LANES
    vmem, smem, dma = pltpu.VMEM, pltpu.SMEM, pltpu.SemaphoreType.DMA
    total = (columns + LEFT + 1) * (height + PAD) + PAD
    padded = (fields, total, LANES)
    anywhere = pl.BlockSpec(memory_space=pl.ANY)
    in_vmem, in_smem = pl.BlockSpec(memory_space=vmem), pl.BlockSpec(memory_space=smem)
    arguments = [
        pltpu.with_memory_space_constraint(x, pltpu.HBM)
        for x in (displacement, spring, stiff_table, match_blocks, match_class)
    ]
    base, rows, index = pl.pallas_call(
        relax,
        out_shape=(vmem(padded, F32), vmem((fields, both, LANES), F32), smem((2, 1, matches), I32)),
        in_specs=[anywhere] * 5,
        out_specs=(in_vmem, in_vmem, in_smem),
        scratch_shapes=[
            vmem(padded, F32),
            vmem((columns, height, LANES), F32),
            vmem((total, LANES), F32), vmem((total, LANES), F32),
            vmem((columns * height, both), BF16),
            vmem((both, both), BF16),
            smem(stiff_table.shape, F32),
            smem((1, matches), I32), smem((1, matches), I32), vmem((2, 1, matches), I32), vmem((2, 1, matches), I32),
            vmem((both, LANES), F32), vmem((both, width), BF16), vmem((both, LANES), F32),
            vmem((2 * columns, both), BF16), vmem((2 * columns, LANES), F32), vmem((both, width), F32),
            vmem((both, LANES), F32),
            vmem((fields, both, LANES), F32),
            vmem((ITERS, fields, both, LANES), F32), vmem((ITERS, fields, both, LANES), F32),
            vmem((2 * both, width), BF16),
            vmem((ITERS, 2, fields * columns, LANES), F32), vmem((ITERS, 2, fields * columns, LANES), F32),
            dma((columns,)), dma((columns,)), dma((4,)), dma((3,)), dma((3,)),
            dma((ITERS, 2, CHUNKS)), dma((ITERS, 2, CHUNKS)), dma((ITERS, 2)), dma((ITERS, 2)),
            pltpu.SemaphoreType.REGULAR,
        ],
        compiler_params=pltpu.CompilerParams(
            collective_id=0, has_side_effects=True, vmem_limit_bytes=48 * 1024 * 1024
        ),
    )(*arguments)
    relaxed, _ = pl.pallas_call(
        finish,
        out_shape=(jax.ShapeDtypeStruct(displacement.shape, F32), vmem(padded, F32)),
        in_specs=[in_vmem, in_vmem, in_smem],
        out_specs=(anywhere, in_vmem),
        scratch_shapes=[dma((columns,))],
        input_output_aliases={0: 1},
        compiler_params=pltpu.CompilerParams(vmem_limit_bytes=24 * 1024 * 1024),
    )(base, rows, index)
    return relaxed


def solution(mesh):
    placed = (
        P(None, "sec", "tile", None),
        P("sec", "tile", None),
        P(),
        P(None, "sec", "tile"),
        P("sec", "tile"),
    )
    return jax.shard_map(
        on_device,
        mesh=mesh,
        in_specs=placed,
        out_specs=P(None, "sec", "tile", None),
        check_vma=False,
    )
```

```python
import jax
import jax.numpy as jnp
from jax import lax
from jax.experimental import pallas as pl
from jax.experimental.pallas import tpu as pltpu
from jax.sharding import PartitionSpec as P

ITERS = 3
LANES = 128
PAD = 8
CHUNKS = 2
LEFT = 2
GROUP = 4
STRIP = 64
MESH = pl.DeviceIdType.MESH
F32 = jnp.float32
BF16 = jnp.bfloat16
I32 = jnp.int32


def split(value):
    high = value.astype(BF16)
    return high, (value - high.astype(F32)).astype(BF16)


def loop(count, body):
    def step(i, carry):
        body(i)
        return carry

    lax.fori_loop(0, count, step, 0)


def relax(
    disp, spring, table_hbm, blocks, classes,
    f_b, last_rows, index,
    f_a, spr, a_ref, g_ref, onehot, pmat,
    table, own_raw, prev_raw, lists_in, lists_own,
    cmat, c_parts, block_cols, edge_hot, edge_g, partial, gathered_g, gathered_l, sent, received, terms,
    edge_out, edge_in,
    load_sem, spring_sem, list_sem, list_send, list_recv,
    row_send, row_recv, edge_send, edge_recv, ready,
):
    fields, _, height, breadth = disp.shape
    columns = breadth // LANES
    stride = height + PAD
    matches = classes.shape[1]
    both = 2 * matches
    part = matches // CHUNKS
    section, sections = lax.axis_index("sec"), lax.axis_size("sec")
    tile, tiles = lax.axis_index("tile"), lax.axis_size("tile")
    has_next, has_prev = section < sections - 1, section > 0
    has_upper, has_lower = tile > 0, tile < tiles - 1
    neighbours = (
        (has_next, {"sec": section + 1}),
        (has_prev, {"sec": section - 1}),
        (has_upper, {"tile": tile - 1}),
        (has_lower, {"tile": tile + 1}),
    )

    shift = columns.bit_length() - 1

    def first_row(cb):
        return pl.multiple_of((cb + LEFT) * stride + PAD, PAD)

    def lanes_of(cb):
        return pl.ds(pl.multiple_of(cb * LANES, LANES), LANES)

    def signal(semaphore, peer):
        pl.semaphore_signal(semaphore, inc=1, device_id=peer, device_id_type=MESH)

    early, late = jnp.logical_and(has_lower, tile % 2 == 1), jnp.logical_and(has_upper, tile % 2 == 0)
    barrier = pltpu.get_barrier_semaphore()
    for i, (there, peer) in enumerate(neighbours):
        greets = jnp.logical_and(there, jnp.logical_not(late)) if i == 2 else there
        pl.when(greets)(lambda peer=peer: signal(barrier, peer))

    own_copies = [
        pltpu.make_async_copy(blocks.at[0], own_raw, list_sem.at[0]),
        pltpu.make_async_copy(blocks.at[0], lists_own.at[0], list_sem.at[1]),
        pltpu.make_async_copy(classes, lists_own.at[1], list_sem.at[2]),
        pltpu.make_async_copy(table_hbm, table, list_sem.at[3]),
    ]
    def load_field(cb):
        return pltpu.make_async_copy(
            disp.at[:, 0, :, lanes_of(cb)], f_a.at[:, pl.ds(first_row(cb), height), :], load_sem.at[cb]
        )

    def load_spring(cb):
        return pltpu.make_async_copy(spring.at[0, :, lanes_of(cb)], spr.at[cb], spring_sem.at[cb])


    for copy in own_copies:
        copy.start()
    loop(columns, lambda cb: load_field(cb).start())

    awaited = [there.astype(I32) for there, _ in neighbours]
    pl.semaphore_wait(barrier, sum(awaited) - early.astype(I32))
    list_copies = [
        pltpu.make_async_remote_copy(
            src_ref=src, dst_ref=dst, send_sem=list_send.at[i], recv_sem=list_recv.at[i],
            device_id={"sec": section + 1}, device_id_type=MESH,
        )
        for i, (src, dst) in enumerate(
            ((blocks.at[1], prev_raw), (blocks.at[1], lists_in.at[0]), (classes, lists_in.at[1]))
        )
    ]

    @pl.when(has_next)
    def _():
        for copy in list_copies:
            copy.start()

    pl.when(late)(lambda: signal(ready, neighbours[2][1]))
    loop(columns, lambda cb: load_spring(cb).start())

    zero_block = jnp.zeros((fields, stride, LANES), F32)
    zero_pad = jnp.zeros((fields, PAD, LANES), F32)
    for field in (f_a, f_b):
        for cb in range(LEFT):
            field[:, cb * stride : (cb + 1) * stride, :] = zero_block
        field[:, (columns + LEFT) * stride + PAD :, :] = zero_block
        field[:, LEFT * stride : LEFT * stride + PAD, :] = zero_pad
        loop(columns, lambda cb: field.__setitem__((slice(None), pl.ds(first_row(cb) + height, PAD), slice(None)), zero_pad))
    for cb in range(LEFT):
        a_ref[cb * stride : (cb + 1) * stride, :] = zero_block[0]
    for there, side in ((has_next, 0), (has_prev, 1)):

        @pl.when(jnp.logical_not(there))
        def _(side=side):
            received[:, :, side * matches : (side + 1) * matches, :] = jnp.zeros((ITERS, fields, matches, LANES), F32)

    def address(block):
        return (block % columns + LEFT) * stride + PAD + block // columns

    def edge_copy(step, way):
        return pltpu.make_async_remote_copy(
            src_ref=edge_out.at[step, way], dst_ref=edge_in.at[step, 1 - way],
            send_sem=edge_send.at[step, way], recv_sem=edge_recv.at[step, 1 - way],
            device_id=neighbours[2 + way][1], device_id_type=MESH,
        )

    def edge_arrival(step, way):
        return pltpu.make_async_remote_copy(
            src_ref=edge_out.at[step, way], dst_ref=edge_in.at[step, way],
            send_sem=edge_send.at[step, way], recv_sem=edge_recv.at[step, way],
            device_id=neighbours[2 + way][1], device_id_type=MESH,
        )

    def row_copy(step, side, chunk, arrival=False):
        mine = side * matches + chunk * part
        theirs = mine if arrival else (1 - side) * matches + chunk * part
        return pltpu.make_async_remote_copy(
            src_ref=sent.at[step, :, pl.ds(mine, part), :],
            dst_ref=received.at[step, :, pl.ds(theirs, part), :],
            send_sem=row_send.at[step, side, chunk],
            recv_sem=row_recv.at[step, side if arrival else 1 - side, chunk],
            device_id=neighbours[side][1], device_id_type=MESH,
        )

    def send_rows(step, side, chunk):
        pl.when(neighbours[side][0])(row_copy(step, side, chunk).start)

    def by_block(side, j):
        block = (own_raw, prev_raw)[side][0, j]
        return ((block & (columns - 1)) + LEFT) * stride + PAD + (block >> shift)

    def by_address(side, j):
        return index[side, 0, j]

    def gather(side, first, count, source, put, find=by_address):
        def group(g):
            at = pl.multiple_of(first + g * 16, 16)
            rows = [source(find(side, at + j)) for j in range(16)]
            for j in range(16):
                put(side * matches + at + j, rows[j])

        loop(count // 16, group)

    def rows_of(ref):
        return lambda at: ref[:, pl.ds(at, 1), :]

    def put_sent(at, row):
        sent[0, :, pl.ds(at, 1), :] = row

    def put_l(at, row):
        gathered_l[:, pl.ds(at, 1), :] = row

    def put_g(at, row):
        gathered_g[pl.ds(at, 1), :] = row

    own_copies[0].wait()
    loop(columns, lambda cb: load_field(cb).wait())
    for chunk in range(CHUNKS):
        gather(0, chunk * part, part, rows_of(f_a), put_sent, by_block)
        send_rows(0, 0, chunk)

    def send_edges(step):
        for way in range(2):
            pl.when(neighbours[2 + way][0])(edge_copy(step, way).start)

    def each_edge(put):
        def one(cb):
            for way in range(2):
                put(way, cb, first_row(cb) + way * (height - 1))

        loop(columns, one)

    def first_edge(way, cb, row):
        for c in range(fields):
            edge_out[0, way, pl.ds(c * columns + cb, 1), :] = f_a[c, pl.ds(row, 1), :]

    each_edge(first_edge)
    for copy in own_copies[1:]:
        copy.wait()
    lists_own[0] = address(lists_own[0])
    own_scalar = pltpu.make_async_copy(lists_own.at[0], index.at[0], list_sem.at[0])
    own_scalar.start()

    def stiffness(lists, alive):
        kind = lists[1]
        stiff = jnp.zeros(kind.shape, F32)
        for level in range(table.shape[0]):
            stiff = jnp.where(kind == level, table[level], stiff)
        return stiff * jnp.where(alive, 1.0, 0.0)

    def place(side, j):
        first = j * LANES // part * 2 * part + side * part + j * LANES % part
        return slice(first, first + LANES)

    def fill_side(side, lists, alive):
        half = pl.ds(side * matches, matches)
        wanted = lists[0]
        stiff = jnp.transpose(jnp.broadcast_to(stiffness(lists, alive), (LANES, matches)))
        cmat[half, :] = stiff
        high, low = split(stiff)
        for j in range(matches // LANES):
            from_rows = slice(j * LANES, (j + 1) * LANES)
            c_parts[place(side, j), 0:LANES] = high[from_rows]
            c_parts[place(side, j), LANES:] = low[from_rows]
        block_cols[half, :] = jnp.transpose(jnp.broadcast_to(wanted.astype(F32), (LANES, matches)))

        def hits(row, j):
            hit = row == wanted[:, j * LANES : (j + 1) * LANES]
            return jnp.where(hit, 1.0, 0.0).astype(BF16)

        def one(cb):
            row = first_row(cb) + lax.broadcasted_iota(I32, (height, LANES), 0)
            at = pl.ds(pl.multiple_of(cb * height, height), height)
            for j in range(matches // LANES):
                onehot[at, place(side, j)] = hits(row, j)

        loop(columns, one)
        order = lax.broadcasted_iota(I32, (2 * columns, LANES), 0)
        row = (order % columns + LEFT) * stride + PAD + order // columns * (height - 1)
        for j in range(matches // LANES):
            edge_hot[:, place(side, j)] = hits(row, j)

    fill_side(0, lists_own, has_next)

    @pl.when(has_prev)
    def _():
        list_copies[0].wait_recv()

    @pl.when(jnp.logical_not(has_prev))
    def _():
        copies = [
            pltpu.make_async_copy(src, dst, list_sem.at[1 + i])
            for i, (src, dst) in enumerate(
                ((blocks.at[1], prev_raw), (blocks.at[1], lists_in.at[0]), (classes, lists_in.at[1]))
            )
        ]
        for copy in copies:
            copy.start()
        for copy in copies:
            copy.wait()

    for chunk in range(CHUNKS):
        gather(1, chunk * part, part, rows_of(f_a), put_sent, by_block)
        send_rows(0, 1, chunk)
    pl.when(early)(lambda: pl.semaphore_wait(ready, 1))
    send_edges(0)

    @pl.when(has_prev)
    def _():
        list_copies[1].wait_recv()
        list_copies[2].wait_recv()

    lists_in[0] = address(lists_in[0])
    prev_scalar = pltpu.make_async_copy(lists_in.at[0], index.at[1], list_sem.at[1])
    prev_scalar.start()
    fill_side(1, lists_in, has_prev)

    def fill_pmat(g):
        at = pl.ds(pl.multiple_of(g * STRIP, STRIP), STRIP)
        col = block_cols[at, :]
        for side, lists in enumerate((lists_own, lists_in)):
            row = lists[0].astype(F32)
            for j in range(matches // LANES):
                hit = jnp.where(col == row[:, j * LANES : (j + 1) * LANES], 1.0, 0.0).astype(BF16)
                pmat[at, place(side, j)] = hit

    loop(both // STRIP, fill_pmat)

    def gains(g):
        at = pl.ds(pl.multiple_of(g * GROUP * height, GROUP * height), GROUP * height)
        sums = jnp.dot(onehot[at, :], c_parts[...], preferred_element_type=F32)
        for w in range(GROUP):
            cb = g * GROUP + w
            here = sums[w * height : (w + 1) * height]
            stiff = spr[cb]
            gain = 0.8 / (4.0 * stiff + (here[:, :LANES] + here[:, LANES:]))
            at = pl.ds(first_row(cb), height)
            g_ref[at, :] = gain
            a_ref[at, :] = gain * stiff

    lane = lax.broadcasted_iota(I32, (STRIP, LANES), 1)

    def stencil(cb, field, result):
        for s in range(height // STRIP):
            top = first_row(cb) + s * STRIP
            at = pl.ds(top, STRIP)
            a = a_ref[at, :]
            for c in range(fields):
                here = field[c, at, :]
                west, east = field[c, pl.ds(top - stride, STRIP), :], field[c, pl.ds(top + stride, STRIP), :]
                north, south = field[c, pl.ds(top - 1, STRIP), :], field[c, pl.ds(top + 1, STRIP), :]
                west = pltpu.roll(jnp.where(lane == LANES - 1, west, here), 1, axis=1)
                east = pltpu.roll(jnp.where(lane == 0, east, here), LANES - 1, axis=1)
                result[c, at, :] = here + a * (((north + south) + (west + east)) - 4.0 * here)

    def add_edges(step, result):
        for way in range(2):

            @pl.when(neighbours[2 + way][0])
            def _(way=way):
                edge_arrival(step, way).wait_recv()

                def one(cb):
                    at = pl.ds(first_row(cb) + way * (height - 1), 1)
                    a = a_ref[at, :]
                    for c in range(fields):
                        result[c, at, :] += a * edge_in[step, way, pl.ds(c * columns + cb, 1), :]

                loop(columns, one)

    def update(g, field):
        at = pl.ds(pl.multiple_of(g * GROUP * height, GROUP * height), GROUP * height)
        sums = jnp.dot(onehot[at, :], terms[0:both, :], preferred_element_type=F32)
        sums = sums + jnp.dot(onehot[at, :], terms[both:, :], preferred_element_type=F32)
        for w in range(GROUP):
            at = pl.ds(first_row(g * GROUP + w), height)
            gain = g_ref[at, :]
            for c in range(fields):
                field[c, at, :] += gain * sums[w * height : (w + 1) * height, c * LANES : (c + 1) * LANES]

    groups = columns // GROUP

    def first_pass(g):
        gains(g + 1)
        for w in range(GROUP):
            stencil(g * GROUP + w, f_a, f_b)

    loop(columns, lambda cb: load_spring(cb).wait())
    gains(0)
    loop(groups - 1, first_pass)
    for w in range(GROUP):
        stencil((groups - 1) * GROUP + w, f_a, f_b)
    own_scalar.wait()
    prev_scalar.wait()
    for side in range(2):
        gather(side, 0, matches, lambda at: g_ref[pl.ds(at, 1), :], put_g)

    def edge_gain(way, cb, row):
        edge_g[pl.ds(way * columns + cb, 1), :] = g_ref[pl.ds(row, 1), :]

    each_edge(edge_gain)

    field, result = f_a, f_b
    for step in range(ITERS):
        last = step == ITERS - 1
        if step > 0:

            def later_pass(g, field=field, result=result):
                update(g + 1, field)
                for w in range(GROUP):
                    stencil(g * GROUP - 1 + w, field, result)

            update(0, field)
            loop(groups - 1, later_pass)
            for w in range(GROUP + 1):
                stencil((groups - 1) * GROUP - 1 + w, field, result)
        add_edges(step, result)
        for side in range(2):
            gather(side, 0, matches, rows_of(result), put_l)
        if not last:

            def edge_base(way, cb, row, step=step, result=result):
                for c in range(fields):
                    edge_out[step + 1, way, pl.ds(c * columns + cb, 1), :] = result[c, pl.ds(row, 1), :]

            each_edge(edge_base)
        for chunk in range(CHUNKS):
            for side in range(2):
                pl.when(neighbours[side][0])(row_copy(step, side, chunk, True).wait_recv)
                at = pl.ds(side * matches + chunk * part, part)
                first = (2 * chunk + side) * part
                c = cmat[at, :]
                for f in range(fields):
                    lanes = slice(f * LANES, (f + 1) * LANES)
                    high, low = split(c * (received[step, f, at, :] - sent[step, f, at, :]))
                    terms[first : first + part, lanes] = high
                    terms[both + first : both + first + part, lanes] = low
            span = slice(2 * chunk * part, 2 * (chunk + 1) * part)
            low_span = slice(both + span.start, both + span.stop)
            for piece in range(CHUNKS):
                for side in range(2):
                    at = pl.ds(side * matches + piece * part, part)
                    sums = jnp.dot(pmat[at, span], terms[span, :], preferred_element_type=F32)
                    sums = sums + jnp.dot(pmat[at, span], terms[low_span, :], preferred_element_type=F32)
                    if chunk > 0:
                        sums = sums + partial[at, :]
                    if chunk < CHUNKS - 1:
                        partial[at, :] = sums
                        continue
                    gain = gathered_g[at, :]
                    for f in range(fields):
                        row = gathered_l[f, at, :] + gain * sums[:, f * LANES : (f + 1) * LANES]
                        if last:
                            last_rows[f, at, :] = row
                        else:
                            sent[step + 1, f, at, :] = row
                    if not last:
                        send_rows(step + 1, side, piece)
        if not last:
            sums = jnp.dot(edge_hot[...], terms[0:both, :], preferred_element_type=F32)
            sums = sums + jnp.dot(edge_hot[...], terms[both:, :], preferred_element_type=F32)
            for way in range(2):
                here = slice(way * columns, (way + 1) * columns)
                gain = edge_g[here, :]
                for c in range(fields):
                    edge_out[step + 1, way, c * columns : (c + 1) * columns, :] += (
                        gain * sums[here, c * LANES : (c + 1) * LANES]
                    )
            send_edges(step + 1)
        field, result = result, field

    @pl.when(has_next)
    def _():
        for copy in list_copies:
            copy.wait_send()

    for step in range(ITERS):
        for way in range(2):
            pl.when(neighbours[2 + way][0])(edge_copy(step, way).wait_send)
        for side in range(2):
            for chunk in range(CHUNKS):
                pl.when(neighbours[side][0])(row_copy(step, side, chunk).wait_send)


def finish(base, rows, index, out, field, out_sem):
    fields, _, height, breadth = out.shape
    columns = breadth // LANES
    stride = height + PAD
    matches = index.shape[2]

    def group(side):
        def one(g):
            at = pl.multiple_of(g * 16, 16)
            got = [rows[:, pl.ds(side * matches + at + j, 1), :] for j in range(16)]
            for j in range(16):
                field[:, pl.ds(index[side, 0, at + j], 1), :] = got[j]

        return one

    for side in range(2):
        loop(matches // 16, group(side))

    def store(cb):
        top = pl.multiple_of((cb + LEFT) * stride + PAD, PAD)
        lanes = pl.ds(pl.multiple_of(cb * LANES, LANES), LANES)
        return pltpu.make_async_copy(field.at[:, pl.ds(top, height), :], out.at[:, 0, :, lanes], out_sem.at[cb])

    loop(columns, lambda cb: store(cb).start())
    loop(columns, lambda cb: store(cb).wait())


def on_device(displacement, spring, stiff_table, match_blocks, match_class):
    fields, _, height, breadth = displacement.shape
    columns = breadth // LANES
    matches = match_class.shape[1]
    both = 2 * matches
    width = fields * LANES
    vmem, smem, dma = pltpu.VMEM, pltpu.SMEM, pltpu.SemaphoreType.DMA
    total = (columns + LEFT + 1) * (height + PAD) + PAD
    padded = (fields, total, LANES)
    anywhere = pl.BlockSpec(memory_space=pl.ANY)
    in_vmem, in_smem = pl.BlockSpec(memory_space=vmem), pl.BlockSpec(memory_space=smem)
    arguments = [
        pltpu.with_memory_space_constraint(x, pltpu.HBM)
        for x in (displacement, spring, stiff_table, match_blocks, match_class)
    ]
    base, rows, index = pl.pallas_call(
        relax,
        out_shape=(vmem(padded, F32), vmem((fields, both, LANES), F32), smem((2, 1, matches), I32)),
        in_specs=[anywhere] * 5,
        out_specs=(in_vmem, in_vmem, in_smem),
        scratch_shapes=[
            vmem(padded, F32),
            vmem((columns, height, LANES), F32),
            vmem((total, LANES), F32), vmem((total, LANES), F32),
            vmem((columns * height, both), BF16),
            vmem((both, both), BF16),
            smem(stiff_table.shape, F32),
            smem((1, matches), I32), smem((1, matches), I32), vmem((2, 1, matches), I32), vmem((2, 1, matches), I32),
            vmem((both, LANES), F32), vmem((both, width), BF16), vmem((both, LANES), F32),
            vmem((2 * columns, both), BF16), vmem((2 * columns, LANES), F32), vmem((both, width), F32),
            vmem((both, LANES), F32),
            vmem((fields, both, LANES), F32),
            vmem((ITERS, fields, both, LANES), F32), vmem((ITERS, fields, both, LANES), F32),
            vmem((2 * both, width), BF16),
            vmem((ITERS, 2, fields * columns, LANES), F32), vmem((ITERS, 2, fields * columns, LANES), F32),
            dma((columns,)), dma((columns,)), dma((4,)), dma((3,)), dma((3,)),
            dma((ITERS, 2, CHUNKS)), dma((ITERS, 2, CHUNKS)), dma((ITERS, 2)), dma((ITERS, 2)),
            pltpu.SemaphoreType.REGULAR,
        ],
        compiler_params=pltpu.CompilerParams(
            collective_id=0, has_side_effects=True, vmem_limit_bytes=48 * 1024 * 1024
        ),
    )(*arguments)
    relaxed, _ = pl.pallas_call(
        finish,
        out_shape=(jax.ShapeDtypeStruct(displacement.shape, F32), vmem(padded, F32)),
        in_specs=[in_vmem, in_vmem, in_smem],
        out_specs=(anywhere, in_vmem),
        scratch_shapes=[dma((columns,))],
        input_output_aliases={0: 1},
        compiler_params=pltpu.CompilerParams(vmem_limit_bytes=24 * 1024 * 1024),
    )(base, rows, index)
    return relaxed


def solution(mesh):
    placed = (
        P(None, "sec", "tile", None),
        P("sec", "tile", None),
        P(),
        P(None, "sec", "tile"),
        P("sec", "tile"),
    )
    return jax.shard_map(
        on_device,
        mesh=mesh,
        in_specs=placed,
        out_specs=P(None, "sec", "tile", None),
        check_vma=False,
    )
```

```python
import jax
import jax.numpy as jnp
from jax import lax
from jax.experimental import pallas as pl
from jax.experimental.pallas import tpu as pltpu
from jax.sharding import PartitionSpec as P

ITERS = 3
LANES = 128
PAD = 8
CHUNKS = 2
LEFT = 2
GROUP = 4
STRIP = 64
MESH = pl.DeviceIdType.MESH
F32 = jnp.float32
BF16 = jnp.bfloat16
I32 = jnp.int32


def split(value):
    high = value.astype(BF16)
    return high, (value - high.astype(F32)).astype(BF16)


def loop(count, body):
    def step(i, carry):
        body(i)
        return carry

    lax.fori_loop(0, count, step, 0)


def relax(
    disp, spring, table_hbm, blocks, classes,
    f_b, last_rows, index,
    f_a, spr, a_ref, g_ref, onehot, pmat,
    table, own_raw, prev_raw, lists_in, lists_own,
    cmat, c_parts, block_cols, edge_hot, edge_g, partial, gathered_g, gathered_l, sent, received, terms,
    edge_out, edge_in,
    load_sem, spring_sem, list_sem, list_send, list_recv,
    row_send, row_recv, edge_send, edge_recv, ready,
):
    fields, _, height, breadth = disp.shape
    columns = breadth // LANES
    stride = height + PAD
    matches = classes.shape[1]
    both = 2 * matches
    part = matches // CHUNKS
    section, sections = lax.axis_index("sec"), lax.axis_size("sec")
    tile, tiles = lax.axis_index("tile"), lax.axis_size("tile")
    has_next, has_prev = section < sections - 1, section > 0
    has_upper, has_lower = tile > 0, tile < tiles - 1
    neighbours = (
        (has_next, {"sec": section + 1}),
        (has_prev, {"sec": section - 1}),
        (has_upper, {"tile": tile - 1}),
        (has_lower, {"tile": tile + 1}),
    )

    shift = columns.bit_length() - 1

    def first_row(cb):
        return pl.multiple_of((cb + LEFT) * stride + PAD, PAD)

    def lanes_of(cb):
        return pl.ds(pl.multiple_of(cb * LANES, LANES), LANES)

    def signal(semaphore, peer):
        pl.semaphore_signal(semaphore, inc=1, device_id=peer, device_id_type=MESH)

    early, late = jnp.logical_and(has_lower, tile % 2 == 1), jnp.logical_and(has_upper, tile % 2 == 0)
    barrier = pltpu.get_barrier_semaphore()
    for i, (there, peer) in enumerate(neighbours):
        greets = jnp.logical_and(there, jnp.logical_not(late)) if i == 2 else there
        pl.when(greets)(lambda peer=peer: signal(barrier, peer))

    own_copies = [
        pltpu.make_async_copy(blocks.at[0], own_raw, list_sem.at[0]),
        pltpu.make_async_copy(blocks.at[0], lists_own.at[0], list_sem.at[1]),
        pltpu.make_async_copy(classes, lists_own.at[1], list_sem.at[2]),
        pltpu.make_async_copy(table_hbm, table, list_sem.at[3]),
    ]
    def load_field(cb):
        return pltpu.make_async_copy(
            disp.at[:, 0, :, lanes_of(cb)], f_a.at[:, pl.ds(first_row(cb), height), :], load_sem.at[cb]
        )

    def load_spring(cb):
        return pltpu.make_async_copy(spring.at[0, :, lanes_of(cb)], spr.at[cb], spring_sem.at[cb])


    for copy in own_copies:
        copy.start()
    loop(columns, lambda cb: load_field(cb).start())
    loop(columns, lambda cb: load_spring(cb).start())

    zero_block = jnp.zeros((fields, stride, LANES), F32)
    zero_pad = jnp.zeros((fields, PAD, LANES), F32)
    for field in (f_a, f_b):
        for cb in range(LEFT):
            field[:, cb * stride : (cb + 1) * stride, :] = zero_block
        field[:, (columns + LEFT) * stride + PAD :, :] = zero_block
        field[:, LEFT * stride : LEFT * stride + PAD, :] = zero_pad
        loop(columns, lambda cb: field.__setitem__((slice(None), pl.ds(first_row(cb) + height, PAD), slice(None)), zero_pad))
    for cb in range(LEFT):
        a_ref[cb * stride : (cb + 1) * stride, :] = zero_block[0]
    for there, side in ((has_next, 0), (has_prev, 1)):

        @pl.when(jnp.logical_not(there))
        def _(side=side):
            received[:, :, side * matches : (side + 1) * matches, :] = jnp.zeros((ITERS, fields, matches, LANES), F32)

    awaited = [there.astype(I32) for there, _ in neighbours]
    pl.semaphore_wait(barrier, sum(awaited) - early.astype(I32))
    list_copies = [
        pltpu.make_async_remote_copy(
            src_ref=src, dst_ref=dst, send_sem=list_send.at[i], recv_sem=list_recv.at[i],
            device_id={"sec": section + 1}, device_id_type=MESH,
        )
        for i, (src, dst) in enumerate(
            ((blocks.at[1], prev_raw), (blocks.at[1], lists_in.at[0]), (classes, lists_in.at[1]))
        )
    ]

    @pl.when(has_next)
    def _():
        for copy in list_copies:
            copy.start()

    pl.when(late)(lambda: signal(ready, neighbours[2][1]))

    def address(block):
        return (block % columns + LEFT) * stride + PAD + block // columns

    def edge_copy(step, way):
        return pltpu.make_async_remote_copy(
            src_ref=edge_out.at[step, way], dst_ref=edge_in.at[step, 1 - way],
            send_sem=edge_send.at[step, way], recv_sem=edge_recv.at[step, 1 - way],
            device_id=neighbours[2 + way][1], device_id_type=MESH,
        )

    def edge_arrival(step, way):
        return pltpu.make_async_remote_copy(
            src_ref=edge_out.at[step, way], dst_ref=edge_in.at[step, way],
            send_sem=edge_send.at[step, way], recv_sem=edge_recv.at[step, way],
            device_id=neighbours[2 + way][1], device_id_type=MESH,
        )

    def row_copy(step, side, chunk, arrival=False):
        mine = side * matches + chunk * part
        theirs = mine if arrival else (1 - side) * matches + chunk * part
        return pltpu.make_async_remote_copy(
            src_ref=sent.at[step, :, pl.ds(mine, part), :],
            dst_ref=received.at[step, :, pl.ds(theirs, part), :],
            send_sem=row_send.at[step, side, chunk],
            recv_sem=row_recv.at[step, side if arrival else 1 - side, chunk],
            device_id=neighbours[side][1], device_id_type=MESH,
        )

    def send_rows(step, side, chunk):
        pl.when(neighbours[side][0])(row_copy(step, side, chunk).start)

    def by_block(side, j):
        block = (own_raw, prev_raw)[side][0, j]
        return ((block & (columns - 1)) + LEFT) * stride + PAD + (block >> shift)

    def by_address(side, j):
        return index[side, 0, j]

    def gather(side, first, count, source, put, find=by_address):
        def group(g):
            at = pl.multiple_of(first + g * 16, 16)
            rows = [source(find(side, at + j)) for j in range(16)]
            for j in range(16):
                put(side * matches + at + j, rows[j])

        loop(count // 16, group)

    def rows_of(ref):
        return lambda at: ref[:, pl.ds(at, 1), :]

    def put_sent(at, row):
        sent[0, :, pl.ds(at, 1), :] = row

    def put_l(at, row):
        gathered_l[:, pl.ds(at, 1), :] = row

    def put_g(at, row):
        gathered_g[pl.ds(at, 1), :] = row

    own_copies[0].wait()
    loop(columns, lambda cb: load_field(cb).wait())
    for chunk in range(CHUNKS):
        gather(0, chunk * part, part, rows_of(f_a), put_sent, by_block)
        send_rows(0, 0, chunk)

    def send_edges(step):
        for way in range(2):
            pl.when(neighbours[2 + way][0])(edge_copy(step, way).start)

    def each_edge(put):
        def one(cb):
            for way in range(2):
                put(way, cb, first_row(cb) + way * (height - 1))

        loop(columns, one)

    def first_edge(way, cb, row):
        for c in range(fields):
            edge_out[0, way, pl.ds(c * columns + cb, 1), :] = f_a[c, pl.ds(row, 1), :]

    each_edge(first_edge)
    for copy in own_copies[1:]:
        copy.wait()
    lists_own[0] = address(lists_own[0])
    own_scalar = pltpu.make_async_copy(lists_own.at[0], index.at[0], list_sem.at[0])
    own_scalar.start()

    def stiffness(lists, alive):
        kind = lists[1]
        stiff = jnp.zeros(kind.shape, F32)
        for level in range(table.shape[0]):
            stiff = jnp.where(kind == level, table[level], stiff)
        return stiff * jnp.where(alive, 1.0, 0.0)

    def place(side, j):
        first = j * LANES // part * 2 * part + side * part + j * LANES % part
        return slice(first, first + LANES)

    def fill_side(side, lists, alive):
        half = pl.ds(side * matches, matches)
        wanted = lists[0]
        stiff = jnp.transpose(jnp.broadcast_to(stiffness(lists, alive), (LANES, matches)))
        cmat[half, :] = stiff
        high, low = split(stiff)
        for j in range(matches // LANES):
            from_rows = slice(j * LANES, (j + 1) * LANES)
            c_parts[place(side, j), 0:LANES] = high[from_rows]
            c_parts[place(side, j), LANES:] = low[from_rows]
        block_cols[half, :] = jnp.transpose(jnp.broadcast_to(wanted.astype(F32), (LANES, matches)))

        def hits(row, j):
            hit = row == wanted[:, j * LANES : (j + 1) * LANES]
            return jnp.where(hit, 1.0, 0.0).astype(BF16)

        def one(cb):
            row = first_row(cb) + lax.broadcasted_iota(I32, (height, LANES), 0)
            at = pl.ds(pl.multiple_of(cb * height, height), height)
            for j in range(matches // LANES):
                onehot[at, place(side, j)] = hits(row, j)

        loop(columns, one)
        order = lax.broadcasted_iota(I32, (2 * columns, LANES), 0)
        row = (order % columns + LEFT) * stride + PAD + order // columns * (height - 1)
        for j in range(matches // LANES):
            edge_hot[:, place(side, j)] = hits(row, j)

    fill_side(0, lists_own, has_next)

    @pl.when(has_prev)
    def _():
        list_copies[0].wait_recv()

    @pl.when(jnp.logical_not(has_prev))
    def _():
        copies = [
            pltpu.make_async_copy(src, dst, list_sem.at[1 + i])
            for i, (src, dst) in enumerate(
                ((blocks.at[1], prev_raw), (blocks.at[1], lists_in.at[0]), (classes, lists_in.at[1]))
            )
        ]
        for copy in copies:
            copy.start()
        for copy in copies:
            copy.wait()

    for chunk in range(CHUNKS):
        gather(1, chunk * part, part, rows_of(f_a), put_sent, by_block)
        send_rows(0, 1, chunk)
    pl.when(early)(lambda: pl.semaphore_wait(ready, 1))
    send_edges(0)

    @pl.when(has_prev)
    def _():
        list_copies[1].wait_recv()
        list_copies[2].wait_recv()

    lists_in[0] = address(lists_in[0])
    prev_scalar = pltpu.make_async_copy(lists_in.at[0], index.at[1], list_sem.at[1])
    prev_scalar.start()
    fill_side(1, lists_in, has_prev)

    def fill_pmat(g):
        at = pl.ds(pl.multiple_of(g * STRIP, STRIP), STRIP)
        col = block_cols[at, :]
        for side, lists in enumerate((lists_own, lists_in)):
            row = lists[0].astype(F32)
            for j in range(matches // LANES):
                hit = jnp.where(col == row[:, j * LANES : (j + 1) * LANES], 1.0, 0.0).astype(BF16)
                pmat[at, place(side, j)] = hit

    loop(both // STRIP, fill_pmat)

    def gains(g):
        at = pl.ds(pl.multiple_of(g * GROUP * height, GROUP * height), GROUP * height)
        sums = jnp.dot(onehot[at, :], c_parts[...], preferred_element_type=F32)
        for w in range(GROUP):
            cb = g * GROUP + w
            here = sums[w * height : (w + 1) * height]
            stiff = spr[cb]
            gain = 0.8 / (4.0 * stiff + (here[:, :LANES] + here[:, LANES:]))
            at = pl.ds(first_row(cb), height)
            g_ref[at, :] = gain
            a_ref[at, :] = gain * stiff

    lane = lax.broadcasted_iota(I32, (STRIP, LANES), 1)

    def stencil(cb, field, result):
        for s in range(height // STRIP):
            top = first_row(cb) + s * STRIP
            at = pl.ds(top, STRIP)
            a = a_ref[at, :]
            for c in range(fields):
                here = field[c, at, :]
                west, east = field[c, pl.ds(top - stride, STRIP), :], field[c, pl.ds(top + stride, STRIP), :]
                north, south = field[c, pl.ds(top - 1, STRIP), :], field[c, pl.ds(top + 1, STRIP), :]
                west = pltpu.roll(jnp.where(lane == LANES - 1, west, here), 1, axis=1)
                east = pltpu.roll(jnp.where(lane == 0, east, here), LANES - 1, axis=1)
                result[c, at, :] = here + a * (((north + south) + (west + east)) - 4.0 * here)

    def add_edges(step, result):
        for way in range(2):

            @pl.when(neighbours[2 + way][0])
            def _(way=way):
                edge_arrival(step, way).wait_recv()

                def one(cb):
                    at = pl.ds(first_row(cb) + way * (height - 1), 1)
                    a = a_ref[at, :]
                    for c in range(fields):
                        result[c, at, :] += a * edge_in[step, way, pl.ds(c * columns + cb, 1), :]

                loop(columns, one)

    def update(g, field):
        at = pl.ds(pl.multiple_of(g * GROUP * height, GROUP * height), GROUP * height)
        sums = jnp.dot(onehot[at, :], terms[0:both, :], preferred_element_type=F32)
        sums = sums + jnp.dot(onehot[at, :], terms[both:, :], preferred_element_type=F32)
        for w in range(GROUP):
            at = pl.ds(first_row(g * GROUP + w), height)
            gain = g_ref[at, :]
            for c in range(fields):
                field[c, at, :] += gain * sums[w * height : (w + 1) * height, c * LANES : (c + 1) * LANES]

    groups = columns // GROUP

    def first_pass(g):
        gains(g + 1)
        for w in range(GROUP):
            stencil(g * GROUP + w, f_a, f_b)

    loop(columns, lambda cb: load_spring(cb).wait())
    gains(0)
    loop(groups - 1, first_pass)
    for w in range(GROUP):
        stencil((groups - 1) * GROUP + w, f_a, f_b)
    own_scalar.wait()
    prev_scalar.wait()
    for side in range(2):
        gather(side, 0, matches, lambda at: g_ref[pl.ds(at, 1), :], put_g)

    def edge_gain(way, cb, row):
        edge_g[pl.ds(way * columns + cb, 1), :] = g_ref[pl.ds(row, 1), :]

    each_edge(edge_gain)

    field, result = f_a, f_b
    for step in range(ITERS):
        last = step == ITERS - 1
        if step > 0:

            def later_pass(g, field=field, result=result):
                update(g + 1, field)
                for w in range(GROUP):
                    stencil(g * GROUP - 1 + w, field, result)

            update(0, field)
            loop(groups - 1, later_pass)
            for w in range(GROUP + 1):
                stencil((groups - 1) * GROUP - 1 + w, field, result)
        add_edges(step, result)
        for side in range(2):
            gather(side, 0, matches, rows_of(result), put_l)
        if not last:

            def edge_base(way, cb, row, step=step, result=result):
                for c in range(fields):
                    edge_out[step + 1, way, pl.ds(c * columns + cb, 1), :] = result[c, pl.ds(row, 1), :]

            each_edge(edge_base)
        for chunk in range(CHUNKS):
            for side in range(2):
                pl.when(neighbours[side][0])(row_copy(step, side, chunk, True).wait_recv)
                at = pl.ds(side * matches + chunk * part, part)
                first = (2 * chunk + side) * part
                c = cmat[at, :]
                for f in range(fields):
                    lanes = slice(f * LANES, (f + 1) * LANES)
                    high, low = split(c * (received[step, f, at, :] - sent[step, f, at, :]))
                    terms[first : first + part, lanes] = high
                    terms[both + first : both + first + part, lanes] = low
            span = slice(2 * chunk * part, 2 * (chunk + 1) * part)
            low_span = slice(both + span.start, both + span.stop)
            for piece in range(CHUNKS):
                for side in range(2):
                    at = pl.ds(side * matches + piece * part, part)
                    sums = jnp.dot(pmat[at, span], terms[span, :], preferred_element_type=F32)
                    sums = sums + jnp.dot(pmat[at, span], terms[low_span, :], preferred_element_type=F32)
                    if chunk > 0:
                        sums = sums + partial[at, :]
                    if chunk < CHUNKS - 1:
                        partial[at, :] = sums
                        continue
                    gain = gathered_g[at, :]
                    for f in range(fields):
                        row = gathered_l[f, at, :] + gain * sums[:, f * LANES : (f + 1) * LANES]
                        if last:
                            last_rows[f, at, :] = row
                        else:
                            sent[step + 1, f, at, :] = row
                    if not last:
                        send_rows(step + 1, side, piece)
        if not last:
            sums = jnp.dot(edge_hot[...], terms[0:both, :], preferred_element_type=F32)
            sums = sums + jnp.dot(edge_hot[...], terms[both:, :], preferred_element_type=F32)
            for way in range(2):
                here = slice(way * columns, (way + 1) * columns)
                gain = edge_g[here, :]
                for c in range(fields):
                    edge_out[step + 1, way, c * columns : (c + 1) * columns, :] += (
                        gain * sums[here, c * LANES : (c + 1) * LANES]
                    )
            send_edges(step + 1)
        field, result = result, field

    @pl.when(has_next)
    def _():
        for copy in list_copies:
            copy.wait_send()

    for step in range(ITERS):
        for way in range(2):
            pl.when(neighbours[2 + way][0])(edge_copy(step, way).wait_send)
        for side in range(2):
            for chunk in range(CHUNKS):
                pl.when(neighbours[side][0])(row_copy(step, side, chunk).wait_send)


def finish(base, rows, index, out, field, out_sem):
    fields, _, height, breadth = out.shape
    columns = breadth // LANES
    stride = height + PAD
    matches = index.shape[2]

    def group(side):
        def one(g):
            at = pl.multiple_of(g * 16, 16)
            got = [rows[:, pl.ds(side * matches + at + j, 1), :] for j in range(16)]
            for j in range(16):
                field[:, pl.ds(index[side, 0, at + j], 1), :] = got[j]

        return one

    for side in range(2):
        loop(matches // 16, group(side))

    def store(cb):
        top = pl.multiple_of((cb + LEFT) * stride + PAD, PAD)
        lanes = pl.ds(pl.multiple_of(cb * LANES, LANES), LANES)
        return pltpu.make_async_copy(field.at[:, pl.ds(top, height), :], out.at[:, 0, :, lanes], out_sem.at[cb])

    loop(columns, lambda cb: store(cb).start())
    loop(columns, lambda cb: store(cb).wait())


def on_device(displacement, spring, stiff_table, match_blocks, match_class):
    fields, _, height, breadth = displacement.shape
    columns = breadth // LANES
    matches = match_class.shape[1]
    both = 2 * matches
    width = fields * LANES
    vmem, smem, dma = pltpu.VMEM, pltpu.SMEM, pltpu.SemaphoreType.DMA
    total = (columns + LEFT + 1) * (height + PAD) + PAD
    padded = (fields, total, LANES)
    anywhere = pl.BlockSpec(memory_space=pl.ANY)
    in_vmem, in_smem = pl.BlockSpec(memory_space=vmem), pl.BlockSpec(memory_space=smem)
    arguments = [
        pltpu.with_memory_space_constraint(x, pltpu.HBM)
        for x in (displacement, spring, stiff_table, match_blocks, match_class)
    ]
    base, rows, index = pl.pallas_call(
        relax,
        out_shape=(vmem(padded, F32), vmem((fields, both, LANES), F32), smem((2, 1, matches), I32)),
        in_specs=[anywhere] * 5,
        out_specs=(in_vmem, in_vmem, in_smem),
        scratch_shapes=[
            vmem(padded, F32),
            vmem((columns, height, LANES), F32),
            vmem((total, LANES), F32), vmem((total, LANES), F32),
            vmem((columns * height, both), BF16),
            vmem((both, both), BF16),
            smem(stiff_table.shape, F32),
            smem((1, matches), I32), smem((1, matches), I32), vmem((2, 1, matches), I32), vmem((2, 1, matches), I32),
            vmem((both, LANES), F32), vmem((both, width), BF16), vmem((both, LANES), F32),
            vmem((2 * columns, both), BF16), vmem((2 * columns, LANES), F32), vmem((both, width), F32),
            vmem((both, LANES), F32),
            vmem((fields, both, LANES), F32),
            vmem((ITERS, fields, both, LANES), F32), vmem((ITERS, fields, both, LANES), F32),
            vmem((2 * both, width), BF16),
            vmem((ITERS, 2, fields * columns, LANES), F32), vmem((ITERS, 2, fields * columns, LANES), F32),
            dma((columns,)), dma((columns,)), dma((4,)), dma((3,)), dma((3,)),
            dma((ITERS, 2, CHUNKS)), dma((ITERS, 2, CHUNKS)), dma((ITERS, 2)), dma((ITERS, 2)),
            pltpu.SemaphoreType.REGULAR,
        ],
        compiler_params=pltpu.CompilerParams(
            collective_id=0, has_side_effects=True, vmem_limit_bytes=48 * 1024 * 1024
        ),
    )(*arguments)
    relaxed, _ = pl.pallas_call(
        finish,
        out_shape=(jax.ShapeDtypeStruct(displacement.shape, F32), vmem(padded, F32)),
        in_specs=[in_vmem, in_vmem, in_smem],
        out_specs=(anywhere, in_vmem),
        scratch_shapes=[dma((columns,))],
        input_output_aliases={0: 1},
        compiler_params=pltpu.CompilerParams(vmem_limit_bytes=24 * 1024 * 1024),
    )(base, rows, index)
    return relaxed


def solution(mesh):
    placed = (
        P(None, "sec", "tile", None),
        P("sec", "tile", None),
        P(),
        P(None, "sec", "tile"),
        P("sec", "tile"),
    )
    return jax.shard_map(
        on_device,
        mesh=mesh,
        in_specs=placed,
        out_specs=P(None, "sec", "tile", None),
        check_vma=False,
    )
```

```python
import jax
import jax.numpy as jnp
from jax import lax
from jax.experimental import pallas as pl
from jax.experimental.pallas import tpu as pltpu
from jax.sharding import PartitionSpec as P

ITERS = 3
LANES = 128
PAD = 8
CHUNKS = 2
LEFT = 2
GROUP = 4
STRIP = 64
MESH = pl.DeviceIdType.MESH
F32 = jnp.float32
BF16 = jnp.bfloat16
I32 = jnp.int32


def split(value):
    high = value.astype(BF16)
    return high, (value - high.astype(F32)).astype(BF16)


def loop(count, body):
    def step(i, carry):
        body(i)
        return carry

    lax.fori_loop(0, count, step, 0)


def relax(
    disp, spring, table_hbm, blocks, classes,
    f_b, last_rows, index,
    f_a, spr, a_ref, g_ref, onehot, pmat,
    table, own_raw, prev_raw, lists_in, lists_own,
    cmat, c_parts, block_cols, edge_hot, edge_g, partial, gathered_g, gathered_l, sent, received, terms,
    edge_out, edge_in,
    load_sem, spring_sem, list_sem, list_send, list_recv,
    row_send, row_recv, edge_send, edge_recv, ready,
):
    fields, _, height, breadth = disp.shape
    columns = breadth // LANES
    stride = height + PAD
    matches = classes.shape[1]
    both = 2 * matches
    part = matches // CHUNKS
    section, sections = lax.axis_index("sec"), lax.axis_size("sec")
    tile, tiles = lax.axis_index("tile"), lax.axis_size("tile")
    has_next, has_prev = section < sections - 1, section > 0
    has_upper, has_lower = tile > 0, tile < tiles - 1
    neighbours = (
        (has_next, {"sec": section + 1}),
        (has_prev, {"sec": section - 1}),
        (has_upper, {"tile": tile - 1}),
        (has_lower, {"tile": tile + 1}),
    )

    shift = columns.bit_length() - 1

    def first_row(cb):
        return pl.multiple_of((cb + LEFT) * stride + PAD, PAD)

    def lanes_of(cb):
        return pl.ds(pl.multiple_of(cb * LANES, LANES), LANES)

    def signal(semaphore, peer):
        pl.semaphore_signal(semaphore, inc=1, device_id=peer, device_id_type=MESH)

    early, late = jnp.logical_and(has_lower, tile % 2 == 1), jnp.logical_and(has_upper, tile % 2 == 0)
    barrier = pltpu.get_barrier_semaphore()
    for i, (there, peer) in enumerate(neighbours):
        greets = jnp.logical_and(there, jnp.logical_not(late)) if i == 2 else there
        pl.when(greets)(lambda peer=peer: signal(barrier, peer))

    own_copies = [
        pltpu.make_async_copy(blocks.at[0], own_raw, list_sem.at[0]),
        pltpu.make_async_copy(blocks.at[0], lists_own.at[0], list_sem.at[1]),
        pltpu.make_async_copy(classes, lists_own.at[1], list_sem.at[2]),
        pltpu.make_async_copy(table_hbm, table, list_sem.at[3]),
    ]
    def load_field(cb):
        return pltpu.make_async_copy(
            disp.at[:, 0, :, lanes_of(cb)], f_a.at[:, pl.ds(first_row(cb), height), :], load_sem.at[cb]
        )

    def load_spring(cb):
        return pltpu.make_async_copy(spring.at[0, :, lanes_of(cb)], spr.at[cb], spring_sem.at[cb])


    for copy in own_copies:
        copy.start()
    loop(columns, lambda cb: load_field(cb).start())
    loop(columns, lambda cb: load_spring(cb).start())

    zero_block = jnp.zeros((fields, stride, LANES), F32)
    zero_pad = jnp.zeros((fields, PAD, LANES), F32)
    for field in (f_a, f_b):
        for cb in range(LEFT):
            field[:, cb * stride : (cb + 1) * stride, :] = zero_block
        field[:, (columns + LEFT) * stride + PAD :, :] = zero_block
        field[:, LEFT * stride : LEFT * stride + PAD, :] = zero_pad
        loop(columns, lambda cb: field.__setitem__((slice(None), pl.ds(first_row(cb) + height, PAD), slice(None)), zero_pad))
    for cb in range(LEFT):
        a_ref[cb * stride : (cb + 1) * stride, :] = zero_block[0]
    for there, side in ((has_next, 0), (has_prev, 1)):

        @pl.when(jnp.logical_not(there))
        def _(side=side):
            received[:, :, side * matches : (side + 1) * matches, :] = jnp.zeros((ITERS, fields, matches, LANES), F32)

    awaited = [there.astype(I32) for there, _ in neighbours]
    pl.semaphore_wait(barrier, sum(awaited) - early.astype(I32))
    list_copies = [
        pltpu.make_async_remote_copy(
            src_ref=src, dst_ref=dst, send_sem=list_send.at[i], recv_sem=list_recv.at[i],
            device_id={"sec": section + 1}, device_id_type=MESH,
        )
        for i, (src, dst) in enumerate(
            ((blocks.at[1], prev_raw), (blocks.at[1], lists_in.at[0]), (classes, lists_in.at[1]))
        )
    ]

    @pl.when(has_next)
    def _():
        list_copies[0].start()

    pl.when(late)(lambda: signal(ready, neighbours[2][1]))

    def address(block):
        return (block % columns + LEFT) * stride + PAD + block // columns

    def edge_copy(step, way):
        return pltpu.make_async_remote_copy(
            src_ref=edge_out.at[step, way], dst_ref=edge_in.at[step, 1 - way],
            send_sem=edge_send.at[step, way], recv_sem=edge_recv.at[step, 1 - way],
            device_id=neighbours[2 + way][1], device_id_type=MESH,
        )

    def edge_arrival(step, way):
        return pltpu.make_async_remote_copy(
            src_ref=edge_out.at[step, way], dst_ref=edge_in.at[step, way],
            send_sem=edge_send.at[step, way], recv_sem=edge_recv.at[step, way],
            device_id=neighbours[2 + way][1], device_id_type=MESH,
        )

    def row_copy(step, side, chunk, arrival=False):
        mine = side * matches + chunk * part
        theirs = mine if arrival else (1 - side) * matches + chunk * part
        return pltpu.make_async_remote_copy(
            src_ref=sent.at[step, :, pl.ds(mine, part), :],
            dst_ref=received.at[step, :, pl.ds(theirs, part), :],
            send_sem=row_send.at[step, side, chunk],
            recv_sem=row_recv.at[step, side if arrival else 1 - side, chunk],
            device_id=neighbours[side][1], device_id_type=MESH,
        )

    def send_rows(step, side, chunk):
        pl.when(neighbours[side][0])(row_copy(step, side, chunk).start)

    def by_block(side, j):
        block = (own_raw, prev_raw)[side][0, j]
        return ((block & (columns - 1)) + LEFT) * stride + PAD + (block >> shift)

    def by_address(side, j):
        return index[side, 0, j]

    def gather(side, first, count, source, put, find=by_address):
        def group(g):
            at = pl.multiple_of(first + g * 16, 16)
            rows = [source(find(side, at + j)) for j in range(16)]
            for j in range(16):
                put(side * matches + at + j, rows[j])

        loop(count // 16, group)

    def rows_of(ref):
        return lambda at: ref[:, pl.ds(at, 1), :]

    def put_sent(at, row):
        sent[0, :, pl.ds(at, 1), :] = row

    def put_l(at, row):
        gathered_l[:, pl.ds(at, 1), :] = row

    def put_g(at, row):
        gathered_g[pl.ds(at, 1), :] = row

    own_copies[0].wait()
    loop(columns, lambda cb: load_field(cb).wait())
    @pl.when(has_next)
    def _():
        for copy in list_copies[1:]:
            copy.start()

    for chunk in range(CHUNKS):
        gather(0, chunk * part, part, rows_of(f_a), put_sent, by_block)
        send_rows(0, 0, chunk)

    def send_edges(step):
        for way in range(2):
            pl.when(neighbours[2 + way][0])(edge_copy(step, way).start)

    def each_edge(put):
        def one(cb):
            for way in range(2):
                put(way, cb, first_row(cb) + way * (height - 1))

        loop(columns, one)

    def first_edge(way, cb, row):
        for c in range(fields):
            edge_out[0, way, pl.ds(c * columns + cb, 1), :] = f_a[c, pl.ds(row, 1), :]

    each_edge(first_edge)
    for copy in own_copies[1:]:
        copy.wait()
    lists_own[0] = address(lists_own[0])
    own_scalar = pltpu.make_async_copy(lists_own.at[0], index.at[0], list_sem.at[0])
    own_scalar.start()

    def stiffness(lists, alive):
        kind = lists[1]
        stiff = jnp.zeros(kind.shape, F32)
        for level in range(table.shape[0]):
            stiff = jnp.where(kind == level, table[level], stiff)
        return stiff * jnp.where(alive, 1.0, 0.0)

    def place(side, j):
        first = j * LANES // part * 2 * part + side * part + j * LANES % part
        return slice(first, first + LANES)

    def fill_side(side, lists, alive):
        half = pl.ds(side * matches, matches)
        wanted = lists[0]
        stiff = jnp.transpose(jnp.broadcast_to(stiffness(lists, alive), (LANES, matches)))
        cmat[half, :] = stiff
        high, low = split(stiff)
        for j in range(matches // LANES):
            from_rows = slice(j * LANES, (j + 1) * LANES)
            c_parts[place(side, j), 0:LANES] = high[from_rows]
            c_parts[place(side, j), LANES:] = low[from_rows]
        block_cols[half, :] = jnp.transpose(jnp.broadcast_to(wanted.astype(F32), (LANES, matches)))

        def hits(row, j):
            hit = row == wanted[:, j * LANES : (j + 1) * LANES]
            return jnp.where(hit, 1.0, 0.0).astype(BF16)

        def one(cb):
            row = first_row(cb) + lax.broadcasted_iota(I32, (height, LANES), 0)
            at = pl.ds(pl.multiple_of(cb * height, height), height)
            for j in range(matches // LANES):
                onehot[at, place(side, j)] = hits(row, j)

        loop(columns, one)
        order = lax.broadcasted_iota(I32, (2 * columns, LANES), 0)
        row = (order % columns + LEFT) * stride + PAD + order // columns * (height - 1)
        for j in range(matches // LANES):
            edge_hot[:, place(side, j)] = hits(row, j)

    fill_side(0, lists_own, has_next)

    @pl.when(has_prev)
    def _():
        list_copies[0].wait_recv()

    @pl.when(jnp.logical_not(has_prev))
    def _():
        copies = [
            pltpu.make_async_copy(src, dst, list_sem.at[1 + i])
            for i, (src, dst) in enumerate(
                ((blocks.at[1], prev_raw), (blocks.at[1], lists_in.at[0]), (classes, lists_in.at[1]))
            )
        ]
        for copy in copies:
            copy.start()
        for copy in copies:
            copy.wait()

    for chunk in range(CHUNKS):
        gather(1, chunk * part, part, rows_of(f_a), put_sent, by_block)
        send_rows(0, 1, chunk)
    pl.when(early)(lambda: pl.semaphore_wait(ready, 1))
    send_edges(0)

    @pl.when(has_prev)
    def _():
        list_copies[1].wait_recv()
        list_copies[2].wait_recv()

    lists_in[0] = address(lists_in[0])
    prev_scalar = pltpu.make_async_copy(lists_in.at[0], index.at[1], list_sem.at[1])
    prev_scalar.start()
    fill_side(1, lists_in, has_prev)

    def fill_pmat(g):
        at = pl.ds(pl.multiple_of(g * STRIP, STRIP), STRIP)
        col = block_cols[at, :]
        for side, lists in enumerate((lists_own, lists_in)):
            row = lists[0].astype(F32)
            for j in range(matches // LANES):
                hit = jnp.where(col == row[:, j * LANES : (j + 1) * LANES], 1.0, 0.0).astype(BF16)
                pmat[at, place(side, j)] = hit

    loop(both // STRIP, fill_pmat)

    def gains(g):
        at = pl.ds(pl.multiple_of(g * GROUP * height, GROUP * height), GROUP * height)
        sums = jnp.dot(onehot[at, :], c_parts[...], preferred_element_type=F32)
        for w in range(GROUP):
            cb = g * GROUP + w
            here = sums[w * height : (w + 1) * height]
            stiff = spr[cb]
            gain = 0.8 / (4.0 * stiff + (here[:, :LANES] + here[:, LANES:]))
            at = pl.ds(first_row(cb), height)
            g_ref[at, :] = gain
            a_ref[at, :] = gain * stiff

    lane = lax.broadcasted_iota(I32, (STRIP, LANES), 1)

    def stencil(cb, field, result):
        for s in range(height // STRIP):
            top = first_row(cb) + s * STRIP
            at = pl.ds(top, STRIP)
            a = a_ref[at, :]
            for c in range(fields):
                here = field[c, at, :]
                west, east = field[c, pl.ds(top - stride, STRIP), :], field[c, pl.ds(top + stride, STRIP), :]
                north, south = field[c, pl.ds(top - 1, STRIP), :], field[c, pl.ds(top + 1, STRIP), :]
                west = pltpu.roll(jnp.where(lane == LANES - 1, west, here), 1, axis=1)
                east = pltpu.roll(jnp.where(lane == 0, east, here), LANES - 1, axis=1)
                result[c, at, :] = here + a * (((north + south) + (west + east)) - 4.0 * here)

    def add_edges(step, result):
        for way in range(2):

            @pl.when(neighbours[2 + way][0])
            def _(way=way):
                edge_arrival(step, way).wait_recv()

                def one(cb):
                    at = pl.ds(first_row(cb) + way * (height - 1), 1)
                    a = a_ref[at, :]
                    for c in range(fields):
                        result[c, at, :] += a * edge_in[step, way, pl.ds(c * columns + cb, 1), :]

                loop(columns, one)

    def update(g, field):
        at = pl.ds(pl.multiple_of(g * GROUP * height, GROUP * height), GROUP * height)
        sums = jnp.dot(onehot[at, :], terms[0:both, :], preferred_element_type=F32)
        sums = sums + jnp.dot(onehot[at, :], terms[both:, :], preferred_element_type=F32)
        for w in range(GROUP):
            at = pl.ds(first_row(g * GROUP + w), height)
            gain = g_ref[at, :]
            for c in range(fields):
                field[c, at, :] += gain * sums[w * height : (w + 1) * height, c * LANES : (c + 1) * LANES]

    groups = columns // GROUP

    def first_pass(g):
        gains(g + 1)
        for w in range(GROUP):
            stencil(g * GROUP + w, f_a, f_b)

    loop(columns, lambda cb: load_spring(cb).wait())
    gains(0)
    loop(groups - 1, first_pass)
    for w in range(GROUP):
        stencil((groups - 1) * GROUP + w, f_a, f_b)
    own_scalar.wait()
    prev_scalar.wait()
    for side in range(2):
        gather(side, 0, matches, lambda at: g_ref[pl.ds(at, 1), :], put_g)

    def edge_gain(way, cb, row):
        edge_g[pl.ds(way * columns + cb, 1), :] = g_ref[pl.ds(row, 1), :]

    each_edge(edge_gain)

    field, result = f_a, f_b
    for step in range(ITERS):
        last = step == ITERS - 1
        if step > 0:

            def later_pass(g, field=field, result=result):
                update(g + 1, field)
                for w in range(GROUP):
                    stencil(g * GROUP - 1 + w, field, result)

            update(0, field)
            loop(groups - 1, later_pass)
            for w in range(GROUP + 1):
                stencil((groups - 1) * GROUP - 1 + w, field, result)
        add_edges(step, result)
        for side in range(2):
            gather(side, 0, matches, rows_of(result), put_l)
        if not last:

            def edge_base(way, cb, row, step=step, result=result):
                for c in range(fields):
                    edge_out[step + 1, way, pl.ds(c * columns + cb, 1), :] = result[c, pl.ds(row, 1), :]

            each_edge(edge_base)
        for chunk in range(CHUNKS):
            for side in range(2):
                pl.when(neighbours[side][0])(row_copy(step, side, chunk, True).wait_recv)
                at = pl.ds(side * matches + chunk * part, part)
                first = (2 * chunk + side) * part
                c = cmat[at, :]
                for f in range(fields):
                    lanes = slice(f * LANES, (f + 1) * LANES)
                    high, low = split(c * (received[step, f, at, :] - sent[step, f, at, :]))
                    terms[first : first + part, lanes] = high
                    terms[both + first : both + first + part, lanes] = low
            span = slice(2 * chunk * part, 2 * (chunk + 1) * part)
            low_span = slice(both + span.start, both + span.stop)
            for piece in range(CHUNKS):
                for side in range(2):
                    at = pl.ds(side * matches + piece * part, part)
                    sums = jnp.dot(pmat[at, span], terms[span, :], preferred_element_type=F32)
                    sums = sums + jnp.dot(pmat[at, span], terms[low_span, :], preferred_element_type=F32)
                    if chunk > 0:
                        sums = sums + partial[at, :]
                    if chunk < CHUNKS - 1:
                        partial[at, :] = sums
                        continue
                    gain = gathered_g[at, :]
                    for f in range(fields):
                        row = gathered_l[f, at, :] + gain * sums[:, f * LANES : (f + 1) * LANES]
                        if last:
                            last_rows[f, at, :] = row
                        else:
                            sent[step + 1, f, at, :] = row
                    if not last:
                        send_rows(step + 1, side, piece)
        if not last:
            sums = jnp.dot(edge_hot[...], terms[0:both, :], preferred_element_type=F32)
            sums = sums + jnp.dot(edge_hot[...], terms[both:, :], preferred_element_type=F32)
            for way in range(2):
                here = slice(way * columns, (way + 1) * columns)
                gain = edge_g[here, :]
                for c in range(fields):
                    edge_out[step + 1, way, c * columns : (c + 1) * columns, :] += (
                        gain * sums[here, c * LANES : (c + 1) * LANES]
                    )
            send_edges(step + 1)
        field, result = result, field

    @pl.when(has_next)
    def _():
        for copy in list_copies:
            copy.wait_send()

    for step in range(ITERS):
        for way in range(2):
            pl.when(neighbours[2 + way][0])(edge_copy(step, way).wait_send)
        for side in range(2):
            for chunk in range(CHUNKS):
                pl.when(neighbours[side][0])(row_copy(step, side, chunk).wait_send)


def finish(base, rows, index, out, field, out_sem):
    fields, _, height, breadth = out.shape
    columns = breadth // LANES
    stride = height + PAD
    matches = index.shape[2]

    def group(side):
        def one(g):
            at = pl.multiple_of(g * 16, 16)
            got = [rows[:, pl.ds(side * matches + at + j, 1), :] for j in range(16)]
            for j in range(16):
                field[:, pl.ds(index[side, 0, at + j], 1), :] = got[j]

        return one

    for side in range(2):
        loop(matches // 16, group(side))

    def store(cb):
        top = pl.multiple_of((cb + LEFT) * stride + PAD, PAD)
        lanes = pl.ds(pl.multiple_of(cb * LANES, LANES), LANES)
        return pltpu.make_async_copy(field.at[:, pl.ds(top, height), :], out.at[:, 0, :, lanes], out_sem.at[cb])

    loop(columns, lambda cb: store(cb).start())
    loop(columns, lambda cb: store(cb).wait())


def on_device(displacement, spring, stiff_table, match_blocks, match_class):
    fields, _, height, breadth = displacement.shape
    columns = breadth // LANES
    matches = match_class.shape[1]
    both = 2 * matches
    width = fields * LANES
    vmem, smem, dma = pltpu.VMEM, pltpu.SMEM, pltpu.SemaphoreType.DMA
    total = (columns + LEFT + 1) * (height + PAD) + PAD
    padded = (fields, total, LANES)
    anywhere = pl.BlockSpec(memory_space=pl.ANY)
    in_vmem, in_smem = pl.BlockSpec(memory_space=vmem), pl.BlockSpec(memory_space=smem)
    arguments = [
        pltpu.with_memory_space_constraint(x, pltpu.HBM)
        for x in (displacement, spring, stiff_table, match_blocks, match_class)
    ]
    base, rows, index = pl.pallas_call(
        relax,
        out_shape=(vmem(padded, F32), vmem((fields, both, LANES), F32), smem((2, 1, matches), I32)),
        in_specs=[anywhere] * 5,
        out_specs=(in_vmem, in_vmem, in_smem),
        scratch_shapes=[
            vmem(padded, F32),
            vmem((columns, height, LANES), F32),
            vmem((total, LANES), F32), vmem((total, LANES), F32),
            vmem((columns * height, both), BF16),
            vmem((both, both), BF16),
            smem(stiff_table.shape, F32),
            smem((1, matches), I32), smem((1, matches), I32), vmem((2, 1, matches), I32), vmem((2, 1, matches), I32),
            vmem((both, LANES), F32), vmem((both, width), BF16), vmem((both, LANES), F32),
            vmem((2 * columns, both), BF16), vmem((2 * columns, LANES), F32), vmem((both, width), F32),
            vmem((both, LANES), F32),
            vmem((fields, both, LANES), F32),
            vmem((ITERS, fields, both, LANES), F32), vmem((ITERS, fields, both, LANES), F32),
            vmem((2 * both, width), BF16),
            vmem((ITERS, 2, fields * columns, LANES), F32), vmem((ITERS, 2, fields * columns, LANES), F32),
            dma((columns,)), dma((columns,)), dma((4,)), dma((3,)), dma((3,)),
            dma((ITERS, 2, CHUNKS)), dma((ITERS, 2, CHUNKS)), dma((ITERS, 2)), dma((ITERS, 2)),
            pltpu.SemaphoreType.REGULAR,
        ],
        compiler_params=pltpu.CompilerParams(
            collective_id=0, has_side_effects=True, vmem_limit_bytes=48 * 1024 * 1024
        ),
    )(*arguments)
    relaxed, _ = pl.pallas_call(
        finish,
        out_shape=(jax.ShapeDtypeStruct(displacement.shape, F32), vmem(padded, F32)),
        in_specs=[in_vmem, in_vmem, in_smem],
        out_specs=(anywhere, in_vmem),
        scratch_shapes=[dma((columns,))],
        input_output_aliases={0: 1},
        compiler_params=pltpu.CompilerParams(vmem_limit_bytes=24 * 1024 * 1024),
    )(base, rows, index)
    return relaxed


def solution(mesh):
    placed = (
        P(None, "sec", "tile", None),
        P("sec", "tile", None),
        P(),
        P(None, "sec", "tile"),
        P("sec", "tile"),
    )
    return jax.shard_map(
        on_device,
        mesh=mesh,
        in_specs=placed,
        out_specs=P(None, "sec", "tile", None),
        check_vma=False,
    )
```
